256 devices in a mesh: resp: 8 (over y, z_hi), prompt: 32 (over x, z_lo, core).
Axes of the slice: x: 4, y: 4, z: 8 (z_hi: 2, z_lo: 4; z = z_hi * 4 + z_lo), core: 2. Of those that a mesh axis runs over, the one named last changes fastest.
Arguments:
- prompt_key_matrix: bfloat16 [512, 512], P('prompt'), may hold values from -4 to 4, as said below
- prompt_value_matrix: bfloat16 [512, 512], P('prompt'), may hold values from -15 to 15
- response_queries: bfloat16 [16, 2048, 2560], P('resp', 'prompt'), may hold values from -4 to 4, as said below
- response_cotangent: bfloat16 [16, 2048, 2560], P('resp', 'prompt'), may hold values from -0.08984375 to 0.08984375
- resp_keys: bfloat16 [16, 2048, 512], P('resp', 'prompt'), may hold values from -4 to 4, as said below
- resp_values: bfloat16 [16, 2048, 512], P('resp', 'prompt'), may hold values from -15 to 15
- thresholds: float32 [16, 2048, 20], P('resp', 'prompt'), may hold values from 0.8 to 1.6, as said below
- lengths: int32 [16], P('resp'), may hold values from 1 to 2048, as said below
Outputs:
- grad_queries: bfloat16 [16, 2048, 2560], P('resp', 'prompt')
- grad_resp_keys: bfloat16 [16, 2048, 512], P('resp', 'prompt')
- grad_resp_values: bfloat16 [16, 2048, 512], P('resp', 'prompt')
- grad_prompt_keys: bfloat16 [512, 512], P('prompt')
- grad_prompt_values: bfloat16 [512, 512], P('prompt')
The draws below stay inside these ranges and needn't reach their ends.
Inputs may be any that keep to these rules, and one draw needn't show every extreme that they name: `prompt_key_matrix`: every entry is a multiple of 1/16. `response_queries`: every entry is a multiple of 1/16. `resp_keys`: every entry is a multiple of 1/16. `thresholds`: each threshold is an odd multiple of 1 / (512 sqrt(128)). `lengths`: in every draw some response has all 2048 positions.
All inputs are finite; a program needn't handle non-finite values.
Results may differ from the reference program's by a relative error of at most 0.024.
Values may be sent and summed in bfloat16 or wider, within the bound.
No kernel may reach another device: no remote copies, remote signals or barrier semaphores. Data moves between devices by JAX's collectives and lax.ppermute only.
A program may use at most 128 MiB of HBM per device.

```python
import math
import jax
import jax.numpy as jnp
from jax import lax

QUERY_HEADS = 20
KEY_VALUE_HEADS = 4
HEAD_DIMENSION = 128
LOCAL_LENGTH = 64
GROUP_RESPONSES = 16
RESPONSE_LENGTH = 2048
PROMPT_TOKENS = 512


def to_grid(values):
    return jnp.clip(jnp.floor(values * 16.0 + 0.5) / 16.0, -4.0, 4.0)


def draw_prompt_key_matrix(key, part):
    key = jax.random.fold_in(key, 11)
    unscaled_scores = jax.random.normal(key, (PROMPT_TOKENS, KEY_VALUE_HEADS * HEAD_DIMENSION), jnp.float32)
    return to_grid(unscaled_scores).astype(jnp.bfloat16)


def draw_response_queries(key, part):
    key = jax.random.fold_in(key, 12)
    unscaled_scores = jax.random.normal(key, (GROUP_RESPONSES, RESPONSE_LENGTH, QUERY_HEADS * HEAD_DIMENSION), jnp.float32)
    return to_grid(unscaled_scores).astype(jnp.bfloat16)


def draw_resp_keys(key, part):
    key = jax.random.fold_in(key, 13)
    unscaled_scores = jax.random.normal(key, (GROUP_RESPONSES, RESPONSE_LENGTH, KEY_VALUE_HEADS * HEAD_DIMENSION), jnp.float32)
    return to_grid(unscaled_scores).astype(jnp.bfloat16)


def draw_prompt_value_matrix(key, part):
    key = jax.random.fold_in(key, 14)
    row_key = jax.random.fold_in(key, 0)
    random_key = jax.random.fold_in(key, 2)
    scales = jnp.exp(jax.random.uniform(row_key, (PROMPT_TOKENS, 1), jnp.float32, math.log(0.3), math.log(3.0)))
    unscaled_scores = jnp.clip(jax.random.normal(random_key, (PROMPT_TOKENS, KEY_VALUE_HEADS * HEAD_DIMENSION), jnp.float32), -5.0, 5.0)
    return (unscaled_scores * scales).astype(jnp.bfloat16)


def draw_resp_values(key, part):
    key = jax.random.fold_in(key, 15)
    row_key = jax.random.fold_in(key, 0)
    random_key = jax.random.fold_in(key, 2)
    scales = jnp.exp(jax.random.uniform(row_key, (GROUP_RESPONSES, RESPONSE_LENGTH, 1), jnp.float32, math.log(0.3), math.log(3.0)))
    unscaled_scores = jnp.clip(jax.random.normal(random_key, (GROUP_RESPONSES, RESPONSE_LENGTH, KEY_VALUE_HEADS * HEAD_DIMENSION), jnp.float32), -5.0, 5.0)
    return (unscaled_scores * scales).astype(jnp.bfloat16)


def draw_thresholds(key, part):
    key = jax.random.fold_in(key, 16)
    root = math.sqrt(HEAD_DIMENSION)
    lowest = math.ceil(204.8 * root)
    highest = math.floor(409.6 * root) - 1
    steps_drawn = jax.random.randint(key, (GROUP_RESPONSES, RESPONSE_LENGTH, QUERY_HEADS), lowest, highest)
    return (2.0 * steps_drawn.astype(jnp.float32) + 1.0) / (512.0 * root)


def draw_lengths(key, part):
    key = jax.random.fold_in(key, 17)
    length_key, pick_key = jax.random.split(key)
    drawn = jax.random.randint(length_key, (GROUP_RESPONSES,), 1, RESPONSE_LENGTH + 1)
    chosen = jax.random.randint(pick_key, (), 0, GROUP_RESPONSES)
    return jnp.where(jnp.arange(GROUP_RESPONSES) == chosen, RESPONSE_LENGTH, drawn).astype(jnp.int32)


def block_levels(own_key, dims, cuts, low, high):
    level, own = 1.0, jax.random.fold_in(own_key, 6)
    for position, blocks in cuts:
        heights = jnp.exp(jax.random.uniform(jax.random.fold_in(own, position), (blocks,), jnp.float32, low / len(cuts), high / len(cuts)))
        level = level * jnp.repeat(heights, dims[position] // blocks).reshape([-1 if axis == position else 1 for axis in range(len(dims))])
    return level


def scatter_about(key, extent, deviation, limit, shards=(), held_as=jnp.bfloat16):
    result = deviation * jax.random.normal(key, extent, jnp.float32)
    if shards:
        result = result * block_levels(key, extent, shards, -0.22, 0.18)
    return jnp.clip(result, -limit, limit).astype(held_as)


def setup_inputs(seed: int = 0) -> dict:
    seeds = jax.random.split(jax.random.key(seed), 9)
    return {
        "prompt_key_matrix": draw_prompt_key_matrix(jax.random.fold_in(seeds[8], 71), 0),
        "prompt_value_matrix": draw_prompt_value_matrix(jax.random.fold_in(seeds[8], 71), 0),
        "response_queries": draw_response_queries(jax.random.fold_in(seeds[8], 71), 0),
        "response_cotangent": scatter_about(seeds[3], (GROUP_RESPONSES, RESPONSE_LENGTH, QUERY_HEADS * HEAD_DIMENSION), 0.015, 0.08984375, ((0, 8), (1, 32))),
        "resp_keys": draw_resp_keys(jax.random.fold_in(seeds[8], 71), 0),
        "resp_values": draw_resp_values(jax.random.fold_in(seeds[8], 71), 0),
        "thresholds": draw_thresholds(jax.random.fold_in(seeds[8], 71), 0),
        "lengths": draw_lengths(jax.random.fold_in(seeds[8], 71), 0),
    }


def to_bf16(values):
    return lax.optimization_barrier(values.astype(jnp.bfloat16)).astype(jnp.float32)


def reference(prompt_key_matrix, prompt_value_matrix, response_queries, response_cotangent, resp_keys, resp_values, thresholds, lengths):
    group_width = QUERY_HEADS // KEY_VALUE_HEADS
    score_scale = HEAD_DIMENSION ** -0.5
    block_widths = KEY_VALUE_HEADS * HEAD_DIMENSION
    prompt_key_grouped = prompt_key_matrix.astype(jnp.float32).reshape(PROMPT_TOKENS, KEY_VALUE_HEADS, HEAD_DIMENSION)
    prompt_value_grouped = prompt_value_matrix.astype(jnp.float32).reshape(PROMPT_TOKENS, KEY_VALUE_HEADS, HEAD_DIMENSION)
    key_pos = jnp.arange(RESPONSE_LENGTH, dtype=jnp.int32)
    prompt_open = jnp.ones((LOCAL_LENGTH, PROMPT_TOKENS), dtype=bool)

    def member_step(outer, member_data):
        prompt_kg, prompt_vg = outer
        query_matrix, output_cotangent, response_key_rows, response_value_rows, member_threshold, length = member_data
        joined_keys = jnp.concatenate([prompt_key_grouped, response_key_rows.astype(jnp.float32).reshape(RESPONSE_LENGTH, KEY_VALUE_HEADS, HEAD_DIMENSION)], 0)
        joined_values = jnp.concatenate([prompt_value_grouped, response_value_rows.astype(jnp.float32).reshape(RESPONSE_LENGTH, KEY_VALUE_HEADS, HEAD_DIMENSION)], 0)

        def block_step(inner, block_index):
            prompt_ksum, prompt_vsum, resp_ksum, resp_vsum = inner
            leading_row = (block_index * LOCAL_LENGTH).astype(jnp.int32)
            positions = leading_row + jnp.arange(LOCAL_LENGTH, dtype=jnp.int32)
            query_tile = lax.dynamic_slice_in_dim(query_matrix, leading_row, LOCAL_LENGTH, 0).astype(jnp.float32).reshape(LOCAL_LENGTH, KEY_VALUE_HEADS, group_width, HEAD_DIMENSION)
            cotangent_block = lax.dynamic_slice_in_dim(output_cotangent, leading_row, LOCAL_LENGTH, 0).astype(jnp.float32).reshape(LOCAL_LENGTH, KEY_VALUE_HEADS, group_width, HEAD_DIMENSION)
            threshold_rows = lax.dynamic_slice_in_dim(member_threshold, leading_row, LOCAL_LENGTH, 0).reshape(LOCAL_LENGTH, KEY_VALUE_HEADS, group_width)
            thresh_block = jnp.transpose(threshold_rows, (1, 2, 0))[..., None]
            scores = jnp.einsum("rghd,kgd->ghrk", query_tile, joined_keys) * score_scale
            own_open = (key_pos[None, :] <= positions[:, None]) & (key_pos[None, :] < length)
            allowed = jnp.concatenate([prompt_open, own_open], 1) & (positions < length)[:, None]
            inside = (scores > thresh_block) & allowed[None, None]
            prob_grad = jnp.einsum("rghd,kgd->ghrk", cotangent_block, joined_values)
            counts = jnp.sum(inside.astype(jnp.float32), -1, keepdims=True)
            grad_mean = jnp.sum(jnp.where(inside, prob_grad, 0.0), -1, keepdims=True) / jnp.maximum(counts, 1.0)
            dscore = to_bf16(jnp.where(inside, prob_grad - grad_mean, 0.0) * score_scale)
            weights = to_bf16(jnp.where(inside, scores - thresh_block, 0.0))
            query_grad = jnp.einsum("ghrk,kgd->rghd", dscore, joined_keys).reshape(LOCAL_LENGTH, QUERY_HEADS * HEAD_DIMENSION).astype(jnp.bfloat16)
            key_grad = jnp.einsum("ghrk,rghd->kgd", dscore, query_tile).reshape(PROMPT_TOKENS + RESPONSE_LENGTH, block_widths)
            value_grad = jnp.einsum("ghrk,rghd->kgd", weights, cotangent_block).reshape(PROMPT_TOKENS + RESPONSE_LENGTH, block_widths)
            state = (prompt_ksum + key_grad[:PROMPT_TOKENS], prompt_vsum + value_grad[:PROMPT_TOKENS],
                     resp_ksum + to_bf16(key_grad[PROMPT_TOKENS:]), resp_vsum + to_bf16(value_grad[PROMPT_TOKENS:]))
            return state, query_grad

        empty_own = jnp.zeros((RESPONSE_LENGTH, block_widths), jnp.float32)
        inner, query_grads = lax.scan(block_step, (prompt_kg, prompt_vg, empty_own, empty_own),
                                      jnp.arange(RESPONSE_LENGTH // LOCAL_LENGTH, dtype=jnp.int32))
        return (inner[0], inner[1]), (query_grads.reshape(RESPONSE_LENGTH, QUERY_HEADS * HEAD_DIMENSION), inner[2].astype(jnp.bfloat16), inner[3].astype(jnp.bfloat16))

    empty_prompt = jnp.zeros((PROMPT_TOKENS, block_widths), jnp.float32)
    totals, produced = lax.scan(member_step, (empty_prompt, empty_prompt),
                                (response_queries, response_cotangent, resp_keys, resp_values, thresholds, lengths))
    grad_queries, grad_resp_keys, grad_resp_values = produced
    return (grad_queries, grad_resp_keys, grad_resp_values,
            totals[0].astype(jnp.bfloat16), totals[1].astype(jnp.bfloat16))
```

```python
import functools

import jax
import jax.numpy as jnp
from jax import lax
from jax.experimental import pallas as pl
from jax.experimental.pallas import tpu as pltpu
from jax.sharding import Mesh
from jax.sharding import PartitionSpec as P

BF = jnp.bfloat16
F32 = jnp.float32
GROUP = 5
HD = 128
OWN = 64
SPAN = 2 * OWN
ROWS = GROUP * SPAN
WIDE = GROUP * HD
PACKED = 2 * WIDE + HD
PROMPT = 512
OWN_PROMPT = 16
KEYS = PROMPT + 2048
ROOT = HD**0.5
NT = (((1,), (1,)), ((), ()))
NN = (((1,), (0,)), ((), ()))
TN = (((0,), (0,)), ((), ()))


def call(body, out_shape, count, scratch=(), limit=None, name=None):
    vm = pl.BlockSpec(memory_space=pltpu.VMEM)
    return pl.pallas_call(
        body,
        out_shape=out_shape,
        in_specs=[pl.BlockSpec(memory_space=pltpu.SMEM)] + [vm] * count,
        out_specs=jax.tree.map(lambda _: vm, out_shape),
        scratch_shapes=scratch,
        compiler_params=pltpu.CompilerParams(vmem_limit_bytes=limit),
        name=name,
    )


def pack_keys_kernel(where, k_ref, v_ref, pk_ref, pv_ref, own_ref, swap_ref):
    x, core = where[0], where[2]
    for s in range(4):
        head = lax.rem(x + s, 4)
        cols = pl.ds(pl.multiple_of(head * HD, HD), HD)
        for out, member in ((own_ref, core), (swap_ref, 1 - core)):
            out[s, 0:OWN, 0:HD] = k_ref[member, :, cols]
            out[s, 0:OWN, HD:] = v_ref[member, :, cols]
            out[s, OWN:, 0:HD] = pk_ref[:, cols]
            out[s, OWN:, HD:] = pv_ref[:, cols]


def pack_rows_kernel(where, q_ref, c_ref, t_ref, *outs):
    x, core = where[0], where[2]
    for s in range(4):
        head = lax.rem(x + s, 4)
        cols = pl.ds(pl.multiple_of(head * WIDE, HD), WIDE)
        for out, member in ((outs[s], core), (outs[4 + s], 1 - core)):
            out[:, 0:WIDE] = q_ref[member, :, cols]
            out[:, WIDE : 2 * WIDE] = c_ref[member, :, cols]
            left = t_ref[member, head]
            for part in range(3):
                piece = left.astype(BF)
                out[:, 2 * WIDE + part * GROUP : 2 * WIDE + (part + 1) * GROUP] = piece
                left = left - piece.astype(F32)
            out[:, 2 * WIDE + 3 * GROUP :] = jnp.zeros((OWN, HD - 3 * GROUP), BF)


def attend_kernel(step, where, *refs):
    own, par, kvs = refs[0:4], refs[4:8], refs[8:12]
    keep, other, grads, prompt_grads = refs[12:16], refs[16:20], refs[20:24], refs[24:28]
    k_all, v_all, qc_all, t_all, q_st, c_st, prob, grad, dk, dv, dq_t, dq_all = refs[28:]
    x, z, core, length = where[0], where[1], where[2], where[3]
    sides = (core, 1 - core)

    def key_places(j):
        zs = lax.rem(z + 4 - j, 4)
        for s in range(4):
            xs = lax.rem(x + 4 - s, 4)
            for side in range(2):
                at = pl.multiple_of(PROMPT + 512 * xs + SPAN * zs + OWN * sides[side], OWN)
                yield s, side, at

    for j in range(4):
        for s, side, at in key_places(j):
            row = s * 160 + side * 80
            k_all[pl.ds(at, OWN)] = kvs[j][row : row + OWN, 0:HD]
            v_all[pl.ds(at, OWN)] = kvs[j][row : row + OWN, HD:]
            slot = j * 128 + s * 32 + side * 16
            k_all[slot : slot + 16] = kvs[j][row + OWN : row + 80, 0:HD]
            v_all[slot : slot + 16] = kvs[j][row + OWN : row + 80, HD:]
    for s in range(4):
        xs = lax.rem(x + 4 - s, 4)
        for side, ref in ((0, own[s]), (1, par[s])):
            qc_all[xs, pl.ds(pl.multiple_of(OWN * sides[side], OWN), OWN)] = ref[...]
    dk[...] = jnp.zeros_like(dk)
    dv[...] = jnp.zeros_like(dv)
    lane = lax.broadcasted_iota(jnp.int32, (1, SPAN), 1)
    sub = lax.broadcasted_iota(jnp.int32, (SPAN, SPAN), 0)
    col = lax.broadcasted_iota(jnp.int32, (SPAN, SPAN), 1)

    def block(b, carry):
        start = b * 512 + z * SPAN

        @pl.when(start >= length)
        def _():
            dq_all[b] = jnp.zeros((SPAN, WIDE), BF)

        @pl.when(start < length)
        def _():
            for h in range(GROUP):
                q_st[h * SPAN : (h + 1) * SPAN] = qc_all[b, :, h * HD : (h + 1) * HD]
                c_st[h * SPAN : (h + 1) * SPAN] = qc_all[b, :, WIDE + h * HD : WIDE + (h + 1) * HD]
            pieces = qc_all[b, :, 2 * WIDE :].astype(F32).T
            t_all[...] = (
                pieces[0:GROUP] + pieces[GROUP : 2 * GROUP] + pieces[2 * GROUP : 3 * GROUP]
            ) * ROOT
            live_row = start + lane < length
            thr = jnp.concatenate(
                [jnp.where(live_row, t_all[h : h + 1], 1e30) for h in range(GROUP)], 1
            )

            def first(k0, count, bar, totals):
                over = (
                    lax.dot_general(
                        k_all[pl.ds(k0, count)], q_st[...], NT, preferred_element_type=F32
                    )
                    - bar
                )
                weight = jnp.maximum(over, 0.0).astype(BF)
                prob[pl.ds(k0, count)] = weight
                pg = lax.dot_general(
                    v_all[pl.ds(k0, count)], c_st[...], NT, preferred_element_type=F32
                )
                grad[pl.ds(k0, count)] = pg
                live = over > 0.0
                num, tot = totals
                num = num + jnp.sum(jnp.where(live, 1.0, 0.0).reshape(count // 8, 8, ROWS), 0)
                tot = tot + jnp.sum(jnp.where(live, pg, 0.0).reshape(count // 8, 8, ROWS), 0)
                dv[pl.ds(k0, count)] += lax.dot_general(
                    weight, c_st[...], NN, preferred_element_type=F32
                )
                return num, tot

            def main(i, totals):
                return first(pl.multiple_of(i * step, step), step, thr, totals)

            base = PROMPT + b * 512

            def tail(i, totals):
                barred = jnp.where(sub + i * SPAN <= col + z * SPAN, 0.0, 1e30)
                bar = thr + jnp.concatenate([barred] * GROUP, 1)
                return first(pl.multiple_of(base + i * SPAN, SPAN), SPAN, bar, totals)

            zero = jnp.zeros((8, ROWS), F32)
            steps = (1 + b) * (512 // step)
            totals = lax.fori_loop(0, steps, main, (zero, zero))
            num, tot = lax.fori_loop(0, z + 1, tail, totals)
            mean = jnp.sum(tot, 0, keepdims=True) / jnp.maximum(
                jnp.sum(num, 0, keepdims=True), 1.0
            )
            dq_t[...] = jnp.zeros_like(dq_t)

            def second(k0, count):
                centred = (grad[pl.ds(k0, count)] - mean).astype(BF)
                ds = jnp.where(prob[pl.ds(k0, count)] > 0, centred, jnp.zeros((), BF))
                dk[pl.ds(k0, count)] += lax.dot_general(
                    ds, q_st[...], NN, preferred_element_type=F32
                )
                dq_t[...] += lax.dot_general(
                    k_all[pl.ds(k0, count)], ds, TN, preferred_element_type=F32
                )

            def main2(i, carry):
                second(pl.multiple_of(i * step, step), step)
                return carry

            def tail2(i, carry):
                second(pl.multiple_of(base + i * SPAN, SPAN), SPAN)
                return carry

            lax.fori_loop(0, steps, main2, 0)
            lax.fori_loop(0, z + 1, tail2, 0)
            for h in range(GROUP):
                dq_all[b, :, h * HD : (h + 1) * HD] = (
                    dq_t[:, h * SPAN : (h + 1) * SPAN].T * (1.0 / ROOT)
                ).astype(BF)

        return carry

    lax.fori_loop(0, 4, block, 0)
    for s in range(4):
        to = lax.rem(x + s, 4)
        for side, ref in ((0, keep[s]), (1, other[s])):
            ref[...] = dq_all[to, pl.ds(pl.multiple_of(OWN * sides[side], OWN), OWN)]
    for j in range(4):
        for part, total in ((0, dk), (1, dv)):
            cols = slice(part * HD, (part + 1) * HD)
            prompt_grads[j][:, cols] = (total[j * 128 : (j + 1) * 128] * (1.0 / ROOT)).astype(BF)
            for s, side, at in key_places(j):
                row = s * SPAN + side * OWN
                grads[j][row : row + OWN, cols] = (total[pl.ds(at, OWN)] * (1.0 / ROOT)).astype(BF)


def unpack_rows_kernel(where, *refs):
    x, core = where[0], where[2]
    out = refs[8]
    for s in range(4):
        head = lax.rem(x + 4 - s, 4)
        cols = pl.ds(pl.multiple_of(head * WIDE, HD), WIDE)
        out[core, :, cols] = refs[s][...]
        out[1 - core, :, cols] = refs[4 + s][...]


def unpack_keys_kernel(where, *refs):
    x, core = where[0], where[2]
    mine, swapped = refs[0:4], refs[4]
    out_k, out_v = refs[5:]
    for s in range(4):
        head = lax.rem(x + s, 4)
        cols = pl.ds(pl.multiple_of(head * HD, HD), HD)
        out_k[core, :, cols] = mine[s][0:OWN, 0:HD]
        out_v[core, :, cols] = mine[s][0:OWN, HD:]
        out_k[1 - core, :, cols] = swapped[s, :, 0:HD]
        out_v[1 - core, :, cols] = swapped[s, :, HD:]


def unpack_prompt_kernel(where, *refs):
    x = where[0]
    mine, swapped = refs[0:4], refs[4]
    out = refs[5]
    for s in range(4):
        head = lax.rem(x + s, 4)
        total = mine[s][0:OWN_PROMPT].astype(F32) + swapped[s].astype(F32)
        for part in range(2):
            cols = pl.ds(pl.multiple_of(part * 4 * HD + head * HD, HD), HD)
            out[:, cols] = total[:, part * HD : (part + 1) * HD]


def shift(values, axis, by):
    by %= 4
    if by == 0:
        return values
    return lax.ppermute(values, axis, [(i, (i + by) % 4) for i in range(4)])


def swap(values):
    return lax.ppermute(values, "core", [(0, 1), (1, 0)])


def shift_swap(values, by):
    pairs = [(2 * i + c, 2 * ((i + by) % 4) + 1 - c) for i in range(4) for c in range(2)]
    return lax.ppermute(values, ("x", "core"), pairs)


def local(
    prompt_key_matrix,
    prompt_value_matrix,
    response_queries,
    response_cotangent,
    resp_keys,
    resp_values,
    thresholds,
    lengths,
):
    x, z, core = lax.axis_index("x"), lax.axis_index("z"), lax.axis_index("core")
    length = lax.dynamic_index_in_dim(lengths, core, 0, keepdims=False)
    where = jnp.stack([x, z, core, length]).astype(jnp.int32)
    shape = jax.ShapeDtypeStruct
    kv_own, kv_swap = call(
        pack_keys_kernel, [shape((4, 80, 2 * HD), BF)] * 2, 4, name="pack_keys"
    )(where, resp_keys, resp_values, prompt_key_matrix, prompt_value_matrix)
    kv_other = swap(kv_swap)
    chip = jnp.concatenate([kv_own, kv_other], 1)
    payload = jnp.concatenate([shift(chip[s], "x", s) for s in range(4)], 0)
    kvs = [shift(payload, "z", j) for j in range(4)]

    thresh = jnp.transpose(thresholds.reshape(2, OWN, 4, GROUP), (0, 2, 1, 3))
    rows = call(pack_rows_kernel, [shape((OWN, PACKED), BF)] * 8, 3, name="pack_rows")(
        where, response_queries, response_cotangent, thresh
    )
    own = [shift(rows[s], "x", s) for s in range(4)]
    par = [shift_swap(rows[4 + s], s) for s in range(4)]

    outs = call(
        functools.partial(attend_kernel, 512),
        [shape((OWN, WIDE), BF)] * 8 + [shape((512, 2 * HD), BF)] * 4 + [shape((128, 2 * HD), BF)] * 4,
        12,
        [
            pltpu.VMEM((KEYS, HD), BF),
            pltpu.VMEM((KEYS, HD), BF),
            pltpu.VMEM((4, SPAN, PACKED), BF),
            pltpu.VMEM((GROUP, SPAN), F32),
            pltpu.VMEM((ROWS, HD), BF),
            pltpu.VMEM((ROWS, HD), BF),
            pltpu.VMEM((KEYS, ROWS), BF),
            pltpu.VMEM((KEYS, ROWS), F32),
            pltpu.VMEM((KEYS, HD), F32),
            pltpu.VMEM((KEYS, HD), F32),
            pltpu.VMEM((HD, ROWS), F32),
            pltpu.VMEM((4, SPAN, WIDE), BF),
        ],
        48 * 1024 * 1024,
        "attend",
    )(where, *own, *par, *kvs)
    keep, other, grads, prompt_grads = outs[0:4], outs[4:8], outs[8:12], outs[12:16]

    def summed(parts):
        got = [shift(parts[j], "z", -j).astype(F32) for j in range(4)]
        return (got[0] + got[1] + got[2] + got[3]).astype(BF)

    prompt_sum = summed(prompt_grads)
    prompt_back = [shift(prompt_sum[32 * s : 32 * s + 32], "x", -s) for s in range(4)]
    prompt_swapped = swap(jnp.stack([p[OWN_PROMPT:] for p in prompt_back]))
    prompt_total = call(unpack_prompt_kernel, shape((OWN_PROMPT, 8 * HD), F32), 5, name="unpack_prompt")(
        where, *prompt_back, prompt_swapped
    )
    for mask in (1, 2, 4):
        prompt_total = prompt_total + lax.ppermute(
            prompt_total, "resp", [(i, i ^ mask) for i in range(8)]
        )
    grad_prompt_keys = prompt_total[:, : 4 * HD].astype(BF)
    grad_prompt_values = prompt_total[:, 4 * HD :].astype(BF)

    back_own = [shift(keep[s], "x", s) for s in range(4)]
    back_par = [shift_swap(other[s], s) for s in range(4)]
    grad_queries = call(unpack_rows_kernel, shape((2, OWN, 4 * WIDE), BF), 8, name="unpack_rows")(
        where, *back_own, *back_par
    )

    key_sum = summed(grads)
    key_back = [shift(key_sum[SPAN * s : SPAN * (s + 1)], "x", -s) for s in range(4)]
    key_swapped = swap(jnp.stack([p[OWN:] for p in key_back]))
    grad_resp_keys, grad_resp_values = call(
        unpack_keys_kernel, [shape((2, OWN, 4 * HD), BF)] * 2, 5, name="unpack_keys"
    )(where, *key_back, key_swapped)
    return (grad_queries, grad_resp_keys, grad_resp_values, grad_prompt_keys, grad_prompt_values)


def solution(mesh):
    fine = Mesh(mesh.devices.reshape(8, 4, 4, 2), ("resp", "x", "z", "core"))
    line = ("x", "z", "core")
    by_row = P("resp", line, None)
    return jax.shard_map(
        local,
        mesh=fine,
        in_specs=(P(line, None), P(line, None), by_row, by_row, by_row, by_row, by_row, P("resp")),
        out_specs=(by_row, by_row, by_row, P(line, None), P(line, None)),
        check_vma=False,
    )
```

```python
import functools

import jax
import jax.numpy as jnp
from jax import lax
from jax.experimental import pallas as pl
from jax.experimental.pallas import tpu as pltpu
from jax.sharding import Mesh
from jax.sharding import PartitionSpec as P

BF = jnp.bfloat16
F32 = jnp.float32
GROUP = 5
HD = 128
OWN = 64
SPAN = 2 * OWN
ROWS = GROUP * SPAN
WIDE = GROUP * HD
PACKED = 2 * WIDE + HD
PROMPT = 512
OWN_PROMPT = 16
KEYS = PROMPT + 2048
ROOT = HD**0.5
NT = (((1,), (1,)), ((), ()))
NN = (((1,), (0,)), ((), ()))
TN = (((0,), (0,)), ((), ()))


def call(body, out_shape, count, scratch=(), limit=None, name=None, scalars=0, flops=1000):
    vm = pl.BlockSpec(memory_space=pltpu.VMEM)
    return pl.pallas_call(
        body,
        out_shape=out_shape,
        in_specs=[pl.BlockSpec(memory_space=pltpu.SMEM)] * scalars + [vm] * count,
        out_specs=jax.tree.map(lambda _: vm, out_shape),
        scratch_shapes=scratch,
        cost_estimate=pl.CostEstimate(flops=flops, bytes_accessed=2 * 10**6, transcendentals=0),
        compiler_params=pltpu.CompilerParams(vmem_limit_bytes=limit),
        name=name,
    )


def pack_keys_kernel(k_ref, v_ref, pk_ref, pv_ref, own_ref, swap_ref):
    x, core = lax.axis_index("x"), lax.axis_index("core")
    for s in range(4):
        head = lax.rem(x + s, 4)
        cols = pl.ds(pl.multiple_of(head * HD, HD), HD)
        for out, member in ((own_ref, core), (swap_ref, 1 - core)):
            out[s, 0:OWN, 0:HD] = k_ref[member, :, cols]
            out[s, 0:OWN, HD:] = v_ref[member, :, cols]
            out[s, OWN:, 0:HD] = pk_ref[:, cols]
            out[s, OWN:, HD:] = pv_ref[:, cols]


def pack_rows_kernel(q_ref, c_ref, t_ref, own_ref, swap_ref):
    x, core = lax.axis_index("x"), lax.axis_index("core")
    for s in range(4):
        head = lax.rem(x + s, 4)
        cols = pl.ds(pl.multiple_of(head * WIDE, HD), WIDE)
        for out, member in ((own_ref, core), (swap_ref, 1 - core)):
            out[s, :, 0:WIDE] = q_ref[member, :, cols]
            out[s, :, WIDE : 2 * WIDE] = c_ref[member, :, cols]
            left = t_ref[member, head]
            for part in range(3):
                piece = left.astype(BF)
                out[s, :, 2 * WIDE + part * GROUP : 2 * WIDE + (part + 1) * GROUP] = piece
                left = left - piece.astype(F32)
            out[s, :, 2 * WIDE + 3 * GROUP :] = jnp.zeros((OWN, HD - 3 * GROUP), BF)


def attend_kernel(step, where, *refs):
    kvs, rows = refs[0:4], refs[4:8]
    grads, prompt_grads, dqs = refs[8:12], refs[12:16], refs[16:20]
    k_all, v_all, qc_all, t_all, q_st, c_st, prob, grad, dk, dv, dq_t, dq_all = refs[20:]
    x, z, core, length = where[0], where[1], where[2], where[3]
    sides = (core, 1 - core)

    def key_places(j):
        zs = lax.rem(z + 4 - j, 4)
        for s in range(4):
            xs = lax.rem(x + 4 - s, 4)
            for side in range(2):
                at = pl.multiple_of(PROMPT + 512 * xs + SPAN * zs + OWN * sides[side], OWN)
                yield s, side, at

    for j in range(4):
        for s, side, at in key_places(j):
            row = s * 160 + side * 80
            k_all[pl.ds(at, OWN)] = kvs[j][row : row + OWN, 0:HD]
            v_all[pl.ds(at, OWN)] = kvs[j][row : row + OWN, HD:]
            slot = j * 128 + s * 32 + side * 16
            k_all[slot : slot + 16] = kvs[j][row + OWN : row + 80, 0:HD]
            v_all[slot : slot + 16] = kvs[j][row + OWN : row + 80, HD:]
    for s in range(4):
        xs = lax.rem(x + 4 - s, 4)
        for side in range(2):
            part = rows[s][side * OWN : (side + 1) * OWN]
            qc_all[xs, pl.ds(pl.multiple_of(OWN * sides[side], OWN), OWN)] = part
    dk[...] = jnp.zeros_like(dk)
    dv[...] = jnp.zeros_like(dv)
    lane = lax.broadcasted_iota(jnp.int32, (1, SPAN), 1)
    sub = lax.broadcasted_iota(jnp.int32, (512, SPAN), 0)
    col = lax.broadcasted_iota(jnp.int32, (512, SPAN), 1)
    barred = jnp.where(sub <= col + z * SPAN, 0.0, 1e30)

    def block(b, carry):
        start = b * 512 + z * SPAN

        @pl.when(start >= length)
        def _():
            dq_all[b] = jnp.zeros((SPAN, WIDE), BF)

        @pl.when(start < length)
        def _():
            for h in range(GROUP):
                q_st[h * SPAN : (h + 1) * SPAN] = qc_all[b, :, h * HD : (h + 1) * HD]
                c_st[h * SPAN : (h + 1) * SPAN] = qc_all[b, :, WIDE + h * HD : WIDE + (h + 1) * HD]
            pieces = qc_all[b, :, 2 * WIDE :].astype(F32).T
            t_all[...] = (
                pieces[0:GROUP] + pieces[GROUP : 2 * GROUP] + pieces[2 * GROUP : 3 * GROUP]
            ) * ROOT
            live_row = start + lane < length
            thr = jnp.concatenate(
                [jnp.where(live_row, t_all[h : h + 1], 1e30) for h in range(GROUP)], 1
            )

            def first(k0, count, bar, totals):
                over = (
                    lax.dot_general(
                        k_all[pl.ds(k0, count)], q_st[...], NT, preferred_element_type=F32
                    )
                    - bar
                )
                weight = jnp.maximum(over, 0.0).astype(BF)
                prob[pl.ds(k0, count)] = weight
                pg = lax.dot_general(
                    v_all[pl.ds(k0, count)], c_st[...], NT, preferred_element_type=F32
                )
                grad[pl.ds(k0, count)] = pg
                live = over > 0.0
                num, tot = totals
                num = num + jnp.sum(jnp.where(live, 1.0, 0.0).reshape(count // 8, 8, ROWS), 0)
                tot = tot + jnp.sum(jnp.where(live, pg, 0.0).reshape(count // 8, 8, ROWS), 0)
                dv[pl.ds(k0, count)] += lax.dot_general(
                    weight, c_st[...], NN, preferred_element_type=F32
                )
                return num, tot

            def main(i, totals):
                return first(pl.multiple_of(i * step, step), step, thr, totals)

            base = PROMPT + b * 512

            def tail(i, totals):
                bar = thr + jnp.concatenate([barred] * GROUP, 1)
                return first(pl.multiple_of(base, 512), 512, bar, totals)

            zero = jnp.zeros((8, ROWS), F32)
            steps = (1 + b) * (512 // step)
            totals = lax.fori_loop(0, steps, main, (zero, zero))
            num, tot = tail(0, totals)
            mean = jnp.sum(tot, 0, keepdims=True) / jnp.maximum(
                jnp.sum(num, 0, keepdims=True), 1.0
            )
            dq_t[...] = jnp.zeros_like(dq_t)

            def second(k0, count):
                centred = (grad[pl.ds(k0, count)] - mean).astype(BF)
                ds = jnp.where(prob[pl.ds(k0, count)] > 0, centred, jnp.zeros((), BF))
                dk[pl.ds(k0, count)] += lax.dot_general(
                    ds, q_st[...], NN, preferred_element_type=F32
                )
                dq_t[...] += lax.dot_general(
                    k_all[pl.ds(k0, count)], ds, TN, preferred_element_type=F32
                )

            def main2(i, carry):
                second(pl.multiple_of(i * step, step), step)
                return carry

            def tail2(i, carry):
                second(pl.multiple_of(base + i * SPAN, SPAN), SPAN)
                return carry

            lax.fori_loop(0, steps, main2, 0)
            second(pl.multiple_of(base, 512), 512)
            for h in range(GROUP):
                dq_all[b, :, h * HD : (h + 1) * HD] = (
                    dq_t[:, h * SPAN : (h + 1) * SPAN].T * (1.0 / ROOT)
                ).astype(BF)

        return carry

    lax.fori_loop(0, 4, block, 0)
    for s in range(4):
        to = lax.rem(x + s, 4)
        for side in range(2):
            part = dq_all[to, pl.ds(pl.multiple_of(OWN * sides[side], OWN), OWN)]
            dqs[s][side * OWN : (side + 1) * OWN] = part
    for j in range(4):
        for part, total in ((0, dk), (1, dv)):
            cols = slice(part * HD, (part + 1) * HD)
            prompt_grads[j][:, cols] = (total[j * 128 : (j + 1) * 128] * (1.0 / ROOT)).astype(BF)
            for s, side, at in key_places(j):
                row = s * SPAN + side * OWN
                grads[j][row : row + OWN, cols] = (total[pl.ds(at, OWN)] * (1.0 / ROOT)).astype(BF)


def attend(where, kvs, rows):
    shape = jax.ShapeDtypeStruct
    return call(
        functools.partial(attend_kernel, 512),
        [shape((512, 2 * HD), BF)] * 4 + [shape((128, 2 * HD), BF)] * 4 + [shape((SPAN, WIDE), BF)] * 4,
        8,
        [
            pltpu.VMEM((KEYS, HD), BF),
            pltpu.VMEM((KEYS, HD), BF),
            pltpu.VMEM((4, SPAN, PACKED), BF),
            pltpu.VMEM((GROUP, SPAN), F32),
            pltpu.VMEM((ROWS, HD), BF),
            pltpu.VMEM((ROWS, HD), BF),
            pltpu.VMEM((KEYS, ROWS), BF),
            pltpu.VMEM((KEYS, ROWS), F32),
            pltpu.VMEM((KEYS, HD), F32),
            pltpu.VMEM((KEYS, HD), F32),
            pltpu.VMEM((HD, ROWS), F32),
            pltpu.VMEM((4, SPAN, WIDE), BF),
        ],
        48 * 1024 * 1024,
        "attend",
        1,
        6 * 10**9,
    )(where, *kvs, *rows)


def unpack_rows_kernel(*refs):
    x, core = lax.axis_index("x"), lax.axis_index("core")
    mine, swapped, out = refs[0:4], refs[4], refs[5]
    for s in range(4):
        head = lax.rem(x + 4 - s, 4)
        cols = pl.ds(pl.multiple_of(head * WIDE, HD), WIDE)
        out[core, :, cols] = mine[s][0:OWN]
        out[1 - core, :, cols] = swapped[s]


def unpack_keys_kernel(*refs):
    x, core = lax.axis_index("x"), lax.axis_index("core")
    mine, swapped = refs[0:4], refs[4]
    out_k, out_v = refs[5:]
    for s in range(4):
        head = lax.rem(x + s, 4)
        cols = pl.ds(pl.multiple_of(head * HD, HD), HD)
        out_k[core, :, cols] = mine[s][0:OWN, 0:HD]
        out_v[core, :, cols] = mine[s][0:OWN, HD:]
        out_k[1 - core, :, cols] = swapped[s, :, 0:HD]
        out_v[1 - core, :, cols] = swapped[s, :, HD:]


def unpack_prompt_kernel(*refs):
    x = lax.axis_index("x")
    mine, swapped = refs[0:4], refs[4]
    out = refs[5]
    for s in range(4):
        head = lax.rem(x + s, 4)
        total = mine[s][0:OWN_PROMPT].astype(F32) + swapped[s].astype(F32)
        for part in range(2):
            cols = pl.ds(pl.multiple_of(part * 4 * HD + head * HD, HD), HD)
            out[:, cols] = total[:, part * HD : (part + 1) * HD]


def shift(values, axis, by):
    by %= 4
    if by == 0:
        return values
    return lax.ppermute(values, axis, [(i, (i + by) % 4) for i in range(4)])


def swap(values):
    return lax.ppermute(values, "core", [(0, 1), (1, 0)])


def local(
    prompt_key_matrix,
    prompt_value_matrix,
    response_queries,
    response_cotangent,
    resp_keys,
    resp_values,
    thresholds,
    lengths,
):
    x, z, core = lax.axis_index("x"), lax.axis_index("z"), lax.axis_index("core")
    length = lax.dynamic_index_in_dim(lengths, core, 0, keepdims=False)
    where = jnp.stack([x, z, core, length]).astype(jnp.int32)
    shape = jax.ShapeDtypeStruct
    kv_own, kv_swap = call(
        pack_keys_kernel, [shape((4, 80, 2 * HD), BF)] * 2, 4, name="pack_keys"
    )(resp_keys, resp_values, prompt_key_matrix, prompt_value_matrix)
    kv_other = swap(kv_swap)
    chip = jnp.concatenate([kv_own, kv_other], 1)
    payload = jnp.concatenate([shift(chip[s], "x", s) for s in range(4)], 0)
    thresh = jnp.transpose(thresholds.reshape(2, OWN, 4, GROUP), (0, 2, 1, 3))
    rows_own, rows_swap = call(
        pack_rows_kernel, [shape((4, OWN, PACKED), BF)] * 2, 3, name="pack_rows"
    )(response_queries, response_cotangent, thresh)
    rows_other = swap(rows_swap)
    rows = [jnp.concatenate([rows_own[s], rows_other[s]], 0) for s in range(4)]
    rows, payload = lax.optimization_barrier((rows, payload))
    kvs = [shift(payload, "z", j) for j in range(4)]
    rows = [shift(rows[s], "x", s) for s in range(4)]
    outs = attend(where, kvs, rows)
    grads, prompt_grads, dqs = outs[0:4], outs[4:8], outs[8:12]

    def summed(parts):
        got = [shift(parts[j], "z", -j).astype(F32) for j in range(4)]
        return (got[0] + got[1] + got[2] + got[3]).astype(BF)

    prompt_sum = summed(prompt_grads)
    dqs, prompt_sum = lax.optimization_barrier((dqs, prompt_sum))
    prompt_back = [shift(prompt_sum[32 * s : 32 * s + 32], "x", -s) for s in range(4)]
    prompt_swapped = swap(jnp.stack([p[OWN_PROMPT:] for p in prompt_back]))
    prompt_total = call(unpack_prompt_kernel, shape((OWN_PROMPT, 8 * HD), F32), 5, name="unpack_prompt")(
        *prompt_back, prompt_swapped
    )
    key_sum = summed(grads)
    key_sum, prompt_total = lax.optimization_barrier((key_sum, prompt_total))
    for mask in (1, 2, 4):
        prompt_total = prompt_total + lax.ppermute(
            prompt_total, "resp", [(i, i ^ mask) for i in range(8)]
        )
    grad_prompt_keys = prompt_total[:, : 4 * HD].astype(BF)
    grad_prompt_values = prompt_total[:, 4 * HD :].astype(BF)

    row_back = [shift(dqs[s], "x", s) for s in range(4)]
    row_swapped = swap(jnp.stack([r[OWN:] for r in row_back]))
    grad_queries = call(unpack_rows_kernel, shape((2, OWN, 4 * WIDE), BF), 5, name="unpack_rows")(
        *row_back, row_swapped
    )

    key_back = [shift(key_sum[SPAN * s : SPAN * (s + 1)], "x", -s) for s in range(4)]
    key_swapped = swap(jnp.stack([p[OWN:] for p in key_back]))
    grad_resp_keys, grad_resp_values = call(
        unpack_keys_kernel, [shape((2, OWN, 4 * HD), BF)] * 2, 5, name="unpack_keys"
    )(*key_back, key_swapped)
    return (grad_queries, grad_resp_keys, grad_resp_values, grad_prompt_keys, grad_prompt_values)


def solution(mesh):
    fine = Mesh(mesh.devices.reshape(8, 4, 4, 2), ("resp", "x", "z", "core"))
    line = ("x", "z", "core")
    by_row = P("resp", line, None)
    return jax.shard_map(
        local,
        mesh=fine,
        in_specs=(P(line, None), P(line, None), by_row, by_row, by_row, by_row, by_row, P("resp")),
        out_specs=(by_row, by_row, by_row, P(line, None), P(line, None)),
        check_vma=False,
    )
```

```python
import functools

import jax
import jax.numpy as jnp
from jax import lax
from jax.experimental import pallas as pl
from jax.experimental.pallas import tpu as pltpu
from jax.sharding import Mesh
from jax.sharding import PartitionSpec as P

BF = jnp.bfloat16
F32 = jnp.float32
GROUP = 5
HD = 128
OWN = 64
SPAN = 2 * OWN
ROWS = GROUP * SPAN
WIDE = GROUP * HD
PACKED = 2 * WIDE + HD
PROMPT = 512
OWN_PROMPT = 16
KEYS = PROMPT + 2048
ROOT = HD**0.5
NT = (((1,), (1,)), ((), ()))
NN = (((1,), (0,)), ((), ()))
TN = (((0,), (0,)), ((), ()))


def call(body, out_shape, count, scratch=(), limit=None, name=None, scalars=0, flops=1000):
    vm = pl.BlockSpec(memory_space=pltpu.VMEM)
    return pl.pallas_call(
        body,
        out_shape=out_shape,
        in_specs=[pl.BlockSpec(memory_space=pltpu.SMEM)] * scalars + [vm] * count,
        out_specs=jax.tree.map(lambda _: vm, out_shape),
        scratch_shapes=scratch,
        cost_estimate=pl.CostEstimate(flops=flops, bytes_accessed=2 * 10**6, transcendentals=0),
        compiler_params=pltpu.CompilerParams(vmem_limit_bytes=limit),
        name=name,
    )


def pack_keys_kernel(k_ref, v_ref, pk_ref, pv_ref, out):
    for head in range(4):
        cols = slice(head * HD, (head + 1) * HD)
        for member in range(2):
            to = 2 * head + member
            out[to, 0:OWN, 0:HD] = k_ref[member, :, cols]
            out[to, 0:OWN, HD:] = v_ref[member, :, cols]
            out[to, OWN:, 0:HD] = pk_ref[:, cols]
            out[to, OWN:, HD:] = pv_ref[:, cols]


def pack_rows_kernel(q_ref, c_ref, t_ref, out):
    for head in range(4):
        cols = slice(head * WIDE, (head + 1) * WIDE)
        for member in range(2):
            to = 2 * head + member
            out[to, :, 0:WIDE] = q_ref[member, :, cols]
            out[to, :, WIDE : 2 * WIDE] = c_ref[member, :, cols]
            left = t_ref[member, head]
            for part in range(3):
                piece = left.astype(BF)
                out[to, :, 2 * WIDE + part * GROUP : 2 * WIDE + (part + 1) * GROUP] = piece
                left = left - piece.astype(F32)
            out[to, :, 2 * WIDE + 3 * GROUP :] = jnp.zeros((OWN, HD - 3 * GROUP), BF)


def attend_kernel(step, where, *refs):
    kvs, rows, grads, prompts, dq = refs[0:4], refs[4], refs[5:9], refs[9:11], refs[11]
    k_all, v_all, t_all, q_st, c_st, prob, grad, dk, dv, dq_t = refs[12:]
    half, core, length = where[0], where[1], where[2]

    def key_places(j):
        far, turned = j // 2, j % 2
        base = 256 * (half if far == 0 else 1 - half) + OWN * (core if turned == 0 else 1 - core)
        for e in range(8):
            at = pl.multiple_of(PROMPT + 512 * (e // 2) + SPAN * (e % 2) + base, OWN)
            yield e, pl.ds(at, OWN), pl.ds(OWN_PROMPT * (8 * j + e), OWN_PROMPT)

    for j in range(4):
        for e, at, slot in key_places(j):
            k_all[at] = kvs[j][e, 0:OWN, 0:HD]
            v_all[at] = kvs[j][e, 0:OWN, HD:]
            k_all[slot] = kvs[j][e, OWN:, 0:HD]
            v_all[slot] = kvs[j][e, OWN:, HD:]
    dk[...] = jnp.zeros_like(dk)
    dv[...] = jnp.zeros_like(dv)
    lane = lax.broadcasted_iota(jnp.int32, (1, SPAN), 1)
    origin = 256 * half + OWN * core
    place = jnp.where(lane < OWN, lane, lane + OWN)
    sub = lax.broadcasted_iota(jnp.int32, (512, SPAN), 0)
    barred = jnp.where(sub <= place + origin, 0.0, 1e30)

    def block(b, carry):
        start = b * 512 + origin

        @pl.when(start >= length)
        def _():
            dq[pl.ds(2 * b, 2)] = jnp.zeros((2, OWN, WIDE), BF)

        @pl.when(start < length)
        def _():
            for side in range(2):
                for h in range(GROUP):
                    to = slice(h * SPAN + side * OWN, h * SPAN + (side + 1) * OWN)
                    q_st[to] = rows[2 * b + side, :, h * HD : (h + 1) * HD]
                    c_st[to] = rows[2 * b + side, :, WIDE + h * HD : WIDE + (h + 1) * HD]
            pieces = jnp.concatenate(
                [rows[2 * b + side, :, 2 * WIDE :].astype(F32) for side in range(2)], 0
            ).T
            t_all[...] = (
                pieces[0:GROUP] + pieces[GROUP : 2 * GROUP] + pieces[2 * GROUP : 3 * GROUP]
            ) * ROOT
            live_row = start + place < length
            thr = jnp.concatenate(
                [jnp.where(live_row, t_all[h : h + 1], 1e30) for h in range(GROUP)], 1
            )

            def first(k0, count, bar, totals):
                over = (
                    lax.dot_general(
                        k_all[pl.ds(k0, count)], q_st[...], NT, preferred_element_type=F32
                    )
                    - bar
                )
                weight = jnp.maximum(over, 0.0).astype(BF)
                prob[pl.ds(k0, count)] = weight
                pg = lax.dot_general(
                    v_all[pl.ds(k0, count)], c_st[...], NT, preferred_element_type=F32
                )
                grad[pl.ds(k0, count)] = pg
                live = over > 0.0
                num, tot = totals
                num = num + jnp.sum(jnp.where(live, 1.0, 0.0).reshape(count // 8, 8, ROWS), 0)
                tot = tot + jnp.sum(jnp.where(live, pg, 0.0).reshape(count // 8, 8, ROWS), 0)
                dv[pl.ds(k0, count)] += lax.dot_general(
                    weight, c_st[...], NN, preferred_element_type=F32
                )
                return num, tot

            def main(i, totals):
                return first(pl.multiple_of(i * step, step), step, thr, totals)

            base = PROMPT + b * 512

            def tail(i, totals):
                bar = thr + jnp.concatenate([barred] * GROUP, 1)
                return first(pl.multiple_of(base, 512), 512, bar, totals)

            zero = jnp.zeros((8, ROWS), F32)
            steps = (1 + b) * (512 // step)
            totals = lax.fori_loop(0, steps, main, (zero, zero))
            num, tot = tail(0, totals)
            mean = jnp.sum(tot, 0, keepdims=True) / jnp.maximum(
                jnp.sum(num, 0, keepdims=True), 1.0
            )
            dq_t[...] = jnp.zeros_like(dq_t)

            def second(k0, count):
                centred = (grad[pl.ds(k0, count)] - mean).astype(BF)
                ds = jnp.where(prob[pl.ds(k0, count)] > 0, centred, jnp.zeros((), BF))
                dk[pl.ds(k0, count)] += lax.dot_general(
                    ds, q_st[...], NN, preferred_element_type=F32
                )
                dq_t[...] += lax.dot_general(
                    k_all[pl.ds(k0, count)], ds, TN, preferred_element_type=F32
                )

            def main2(i, carry):
                second(pl.multiple_of(i * step, step), step)
                return carry

            def tail2(i, carry):
                second(pl.multiple_of(base + i * SPAN, SPAN), SPAN)
                return carry

            lax.fori_loop(0, steps, main2, 0)
            second(pl.multiple_of(base, 512), 512)
            for h in range(GROUP):
                part = (dq_t[:, h * SPAN : (h + 1) * SPAN].T * (1.0 / ROOT)).astype(BF)
                for side in range(2):
                    dq[2 * b + side, :, h * HD : (h + 1) * HD] = part[side * OWN : (side + 1) * OWN]

        return carry

    lax.fori_loop(0, 4, block, 0)
    for j in range(4):
        for part, total in ((0, dk), (1, dv)):
            cols = slice(part * HD, (part + 1) * HD)
            for e, at, slot in key_places(j):
                grads[j][e, :, cols] = (total[at] * (1.0 / ROOT)).astype(BF)
            held = (total[128 * j : 128 * (j + 1)] * (1.0 / ROOT)).astype(BF)
            prompts[j % 2][j // 2 * 128 : (j // 2 + 1) * 128, cols] = held


def attend(where, kvs, rows):
    shape = jax.ShapeDtypeStruct
    return call(
        functools.partial(attend_kernel, 512),
        [shape((8, OWN, 2 * HD), BF)] * 4
        + [shape((256, 2 * HD), BF)] * 2
        + [shape((8, OWN, WIDE), BF)],
        5,
        [
            pltpu.VMEM((KEYS, HD), BF),
            pltpu.VMEM((KEYS, HD), BF),
            pltpu.VMEM((GROUP, SPAN), F32),
            pltpu.VMEM((ROWS, HD), BF),
            pltpu.VMEM((ROWS, HD), BF),
            pltpu.VMEM((KEYS, ROWS), BF),
            pltpu.VMEM((KEYS, ROWS), F32),
            pltpu.VMEM((KEYS, HD), F32),
            pltpu.VMEM((KEYS, HD), F32),
            pltpu.VMEM((HD, ROWS), F32),
        ],
        48 * 1024 * 1024,
        "attend",
        1,
        6 * 10**9,
    )(where, *kvs, rows)


def unpack_rows_kernel(got, out_q, out_k, out_v):
    for head in range(4):
        cols = slice(head * HD, (head + 1) * HD)
        for member in range(2):
            part = got.at[2 * head + member]
            out_q[member, :, head * WIDE : (head + 1) * WIDE] = part[:, 0:WIDE]
            out_k[member, :, cols] = part[:, WIDE : WIDE + HD]
            out_v[member, :, cols] = part[:, WIDE + HD :]


def unpack_prompt_kernel(got, out_k, out_v):
    for head in range(4):
        cols = slice(head * HD, (head + 1) * HD)
        total = got[2 * head].astype(F32) + got[2 * head + 1].astype(F32)
        out_k[:, cols] = total[:, 0:HD].astype(BF)
        out_v[:, cols] = total[:, HD:].astype(BF)


def swap(values):
    return lax.ppermute(values, "core", [(0, 1), (1, 0)])


def far(values):
    return lax.ppermute(values, "half", [(0, 1), (1, 0)])


def exchange(values):
    return lax.all_to_all(values, ("x", "near"), 0, 0, tiled=True)


def added(*parts):
    return functools.reduce(jnp.add, [p.astype(F32) for p in parts]).astype(BF)


def local(
    prompt_key_matrix,
    prompt_value_matrix,
    response_queries,
    response_cotangent,
    resp_keys,
    resp_values,
    thresholds,
    lengths,
):
    half, near, core = (lax.axis_index(name) for name in ("half", "near", "core"))
    length = lax.dynamic_index_in_dim(lengths, near, 0, keepdims=False)
    where = jnp.stack([half, core, length]).astype(jnp.int32)
    shape = jax.ShapeDtypeStruct
    packed = call(pack_keys_kernel, shape((8, 80, 2 * HD), BF), 4, name="pack_keys")(
        resp_keys, resp_values, prompt_key_matrix, prompt_value_matrix
    )
    keys_own = exchange(packed)
    thresh = jnp.transpose(thresholds.reshape(2, OWN, 4, GROUP), (0, 2, 1, 3))
    rows = call(pack_rows_kernel, shape((8, OWN, PACKED), BF), 3, name="pack_rows")(
        response_queries, response_cotangent, thresh
    )
    keys_far = far(keys_own)
    rows = exchange(rows)
    kvs = [keys_own, swap(keys_own), keys_far, swap(keys_far)]
    outs = attend(where, kvs, rows)
    grads, prompts, dq = outs[0:4], outs[4:6], outs[6]

    far_sum = added(grads[2], swap(grads[3]))
    prompt_sum = added(prompts[0], swap(prompts[1]))
    key_sum = added(grads[0], swap(grads[1]), far(far_sum))
    corners = [
        lax.ppermute(part, ("hi", "half"), [(i, i ^ mask) for i in range(4)])
        for part, mask in ((prompt_sum[:128], 2), (prompt_sum[128:], 1), (prompt_sum[128:], 3))
    ]
    prompt_sum = added(prompt_sum[:128], *corners)
    key_sum, prompt_sum = lax.optimization_barrier((key_sum, prompt_sum))
    back = exchange(jnp.concatenate([dq, key_sum], 2))
    around = [
        lax.ppermute(prompt_sum, "y", [(i, (i + by) % 4) for i in range(4)]) for by in (1, 2, 3)
    ]
    prompt_sum = added(prompt_sum, *around).reshape(8, OWN_PROMPT, 2 * HD)
    back, prompt_sum = lax.optimization_barrier((back, prompt_sum))
    prompt_back = exchange(prompt_sum)
    grad_queries, grad_resp_keys, grad_resp_values = call(
        unpack_rows_kernel,
        [shape((2, OWN, 4 * WIDE), BF)] + [shape((2, OWN, 4 * HD), BF)] * 2,
        1,
        name="unpack_rows",
    )(back)
    grad_prompt_keys, grad_prompt_values = call(
        unpack_prompt_kernel, [shape((OWN_PROMPT, 4 * HD), BF)] * 2, 1, name="unpack_prompt"
    )(prompt_back)
    return (grad_queries, grad_resp_keys, grad_resp_values, grad_prompt_keys, grad_prompt_values)


def solution(mesh):
    axes = ("y", "hi", "x", "half", "near", "core")
    fine = Mesh(mesh.devices.reshape(4, 2, 4, 2, 2, 2), axes)
    group, line = axes[:2], axes[2:]
    by_row = P(group, line, None)
    return jax.shard_map(
        local,
        mesh=fine,
        in_specs=(P(line, None), P(line, None), by_row, by_row, by_row, by_row, by_row, P(group)),
        out_specs=(by_row, by_row, by_row, P(line, None), P(line, None)),
        check_vma=False,
    )
```

```python
import functools

import jax
import jax.numpy as jnp
from jax import lax
from jax.experimental import pallas as pl
from jax.experimental.pallas import tpu as pltpu
from jax.sharding import Mesh
from jax.sharding import PartitionSpec as P

BF = jnp.bfloat16
F32 = jnp.float32
GROUP = 5
HD = 128
OWN = 64
SPAN = 2 * OWN
ROWS = GROUP * SPAN
WIDE = GROUP * HD
PACKED = 2 * WIDE + HD
PROMPT = 512
OWN_PROMPT = 16
KEYS = PROMPT + 2048
ROOT = HD**0.5
NT = (((1,), (1,)), ((), ()))
NN = (((1,), (0,)), ((), ()))
TN = (((0,), (0,)), ((), ()))


def call(body, out_shape, count, scratch=(), limit=None, name=None, scalars=0, flops=1000):
    vm = pl.BlockSpec(memory_space=pltpu.VMEM)
    return pl.pallas_call(
        body,
        out_shape=out_shape,
        in_specs=[pl.BlockSpec(memory_space=pltpu.SMEM)] * scalars + [vm] * count,
        out_specs=jax.tree.map(lambda _: vm, out_shape),
        scratch_shapes=scratch,
        cost_estimate=pl.CostEstimate(flops=flops, bytes_accessed=2 * 10**6, transcendentals=0),
        compiler_params=pltpu.CompilerParams(vmem_limit_bytes=limit),
        name=name,
    )


def pack_keys_kernel(k_ref, v_ref, pk_ref, pv_ref, out):
    for head in range(4):
        cols = slice(head * HD, (head + 1) * HD)
        for member in range(2):
            to = 2 * head + member
            out[to, 0:OWN, 0:HD] = k_ref[member, :, cols]
            out[to, 0:OWN, HD:] = v_ref[member, :, cols]
            out[to, OWN:, 0:HD] = pk_ref[:, cols]
            out[to, OWN:, HD:] = pv_ref[:, cols]


def pack_rows_kernel(q_ref, c_ref, t_ref, out):
    for head in range(4):
        cols = slice(head * WIDE, (head + 1) * WIDE)
        for member in range(2):
            to = 2 * head + member
            out[to, :, 0:WIDE] = q_ref[member, :, cols]
            out[to, :, WIDE : 2 * WIDE] = c_ref[member, :, cols]
            left = t_ref[member, head]
            for part in range(3):
                piece = left.astype(BF)
                out[to, :, 2 * WIDE + part * GROUP : 2 * WIDE + (part + 1) * GROUP] = piece
                left = left - piece.astype(F32)
            out[to, :, 2 * WIDE + 3 * GROUP :] = jnp.zeros((OWN, HD - 3 * GROUP), BF)


def attend_kernel(step, where, *refs):
    kvs, rows, grads, dq = refs[0:4], refs[4], refs[5:9], refs[9]
    k_all, v_all, t_all, q_st, c_st, prob, grad, dk, dv, dq_t = refs[10:]
    half, core, length = where[0], where[1], where[2]

    def key_places(j):
        far, turned = j // 2, j % 2
        base = 256 * (half if far == 0 else 1 - half) + OWN * (core if turned == 0 else 1 - core)
        for e in range(8):
            at = pl.multiple_of(PROMPT + 512 * (e // 2) + SPAN * (e % 2) + base, OWN)
            yield e, pl.ds(at, OWN), pl.ds(OWN_PROMPT * (8 * j + e), OWN_PROMPT)

    for j in range(4):
        for e, at, slot in key_places(j):
            k_all[at] = kvs[j][e, 0:OWN, 0:HD]
            v_all[at] = kvs[j][e, 0:OWN, HD:]
            k_all[slot] = kvs[j][e, OWN:, 0:HD]
            v_all[slot] = kvs[j][e, OWN:, HD:]
    dk[...] = jnp.zeros_like(dk)
    dv[...] = jnp.zeros_like(dv)
    lane = lax.broadcasted_iota(jnp.int32, (1, SPAN), 1)
    origin = 256 * half + OWN * core
    place = jnp.where(lane < OWN, lane, lane + OWN)
    sub = lax.broadcasted_iota(jnp.int32, (512, SPAN), 0)
    barred = jnp.where(sub <= place + origin, 0.0, 1e30)

    def block(b, carry):
        start = b * 512 + origin

        @pl.when(start >= length)
        def _():
            dq[pl.ds(2 * b, 2)] = jnp.zeros((2, OWN, WIDE), BF)

        @pl.when(start < length)
        def _():
            for side in range(2):
                for h in range(GROUP):
                    to = slice(h * SPAN + side * OWN, h * SPAN + (side + 1) * OWN)
                    q_st[to] = rows[2 * b + side, :, h * HD : (h + 1) * HD]
                    c_st[to] = rows[2 * b + side, :, WIDE + h * HD : WIDE + (h + 1) * HD]
            pieces = jnp.concatenate(
                [rows[2 * b + side, :, 2 * WIDE :].astype(F32) for side in range(2)], 0
            ).T
            t_all[...] = (
                pieces[0:GROUP] + pieces[GROUP : 2 * GROUP] + pieces[2 * GROUP : 3 * GROUP]
            ) * ROOT
            live_row = start + place < length
            thr = jnp.concatenate(
                [jnp.where(live_row, t_all[h : h + 1], 1e30) for h in range(GROUP)], 1
            )

            def first(k0, count, bar, totals):
                over = (
                    lax.dot_general(
                        k_all[pl.ds(k0, count)], q_st[...], NT, preferred_element_type=F32
                    )
                    - bar
                )
                weight = jnp.maximum(over, 0.0).astype(BF)
                prob[pl.ds(k0, count)] = weight
                pg = lax.dot_general(
                    v_all[pl.ds(k0, count)], c_st[...], NT, preferred_element_type=F32
                )
                grad[pl.ds(k0, count)] = pg
                live = over > 0.0
                num, tot = totals
                num = num + jnp.sum(jnp.where(live, 1.0, 0.0).reshape(count // 8, 8, ROWS), 0)
                tot = tot + jnp.sum(jnp.where(live, pg, 0.0).reshape(count // 8, 8, ROWS), 0)
                dv[pl.ds(k0, count)] += lax.dot_general(
                    weight, c_st[...], NN, preferred_element_type=F32
                )
                return num, tot

            def main(i, totals):
                return first(pl.multiple_of(i * 2 * step, 2 * step), 2 * step, thr, totals)

            base = PROMPT + b * 512

            def tail(i, totals):
                bar = thr + jnp.concatenate([barred] * GROUP, 1)
                return first(pl.multiple_of(base, 512), 512, bar, totals)

            zero = jnp.zeros((8, ROWS), F32)
            pairs = (1 + b) // 2
            odd = (1 + b) - 2 * pairs
            last = pl.multiple_of(pairs * 2 * step, 2 * step)
            totals = lax.fori_loop(0, pairs, main, (zero, zero))
            totals = lax.fori_loop(0, odd, lambda i, t: first(last, step, thr, t), totals)
            num, tot = tail(0, totals)
            mean = jnp.sum(tot, 0, keepdims=True) / jnp.maximum(
                jnp.sum(num, 0, keepdims=True), 1.0
            )
            dq_t[...] = jnp.zeros_like(dq_t)

            def second(k0, count):
                centred = (grad[pl.ds(k0, count)] - mean).astype(BF)
                ds = jnp.where(prob[pl.ds(k0, count)] > 0, centred, jnp.zeros((), BF))
                dk[pl.ds(k0, count)] += lax.dot_general(
                    ds, q_st[...], NN, preferred_element_type=F32
                )
                dq_t[...] += lax.dot_general(
                    k_all[pl.ds(k0, count)], ds, TN, preferred_element_type=F32
                )

            def main2(i, carry):
                second(pl.multiple_of(i * 2 * step, 2 * step), 2 * step)
                return carry

            def odd2(i, carry):
                second(last, step)
                return carry

            lax.fori_loop(0, pairs, main2, 0)
            lax.fori_loop(0, odd, odd2, 0)
            second(pl.multiple_of(base, 512), 512)
            for h in range(GROUP):
                part = (dq_t[:, h * SPAN : (h + 1) * SPAN].T * (1.0 / ROOT)).astype(BF)
                for side in range(2):
                    dq[2 * b + side, :, h * HD : (h + 1) * HD] = part[side * OWN : (side + 1) * OWN]

        return carry

    lax.fori_loop(0, 4, block, 0)
    for j in range(4):
        for part, total in ((0, dk), (1, dv)):
            cols = slice(part * HD, (part + 1) * HD)
            for e, at, slot in key_places(j):
                grads[j][e, 0:OWN, cols] = (total[at] * (1.0 / ROOT)).astype(BF)
                grads[j][e, OWN:, cols] = (total[slot] * (1.0 / ROOT)).astype(BF)


def attend(where, kvs, rows):
    shape = jax.ShapeDtypeStruct
    return call(
        functools.partial(attend_kernel, 512),
        [shape((8, 80, 2 * HD), BF)] * 4 + [shape((8, OWN, WIDE), BF)],
        5,
        [
            pltpu.VMEM((KEYS, HD), BF),
            pltpu.VMEM((KEYS, HD), BF),
            pltpu.VMEM((GROUP, SPAN), F32),
            pltpu.VMEM((ROWS, HD), BF),
            pltpu.VMEM((ROWS, HD), BF),
            pltpu.VMEM((KEYS, ROWS), BF),
            pltpu.VMEM((KEYS, ROWS), F32),
            pltpu.VMEM((KEYS, HD), F32),
            pltpu.VMEM((KEYS, HD), F32),
            pltpu.VMEM((HD, ROWS), F32),
        ],
        48 * 1024 * 1024,
        "attend",
        1,
        6 * 10**9,
    )(where, *kvs, rows)


def unpack_rows_kernel(got, out_q, out_k, out_v):
    for head in range(4):
        cols = slice(head * HD, (head + 1) * HD)
        for member in range(2):
            part = got.at[2 * head + member]
            out_q[member, :, head * WIDE : (head + 1) * WIDE] = part[:, 0:WIDE]
            out_k[member, :, cols] = part[:, WIDE : WIDE + HD]
            out_v[member, :, cols] = part[:, WIDE + HD :]


def unpack_prompt_kernel(got, out_k, out_v):
    for head in range(4):
        cols = slice(head * HD, (head + 1) * HD)
        total = got[2 * head].astype(F32) + got[2 * head + 1].astype(F32)
        out_k[:, cols] = total[:, 0:HD].astype(BF)
        out_v[:, cols] = total[:, HD:].astype(BF)


def swap(values):
    return lax.ppermute(values, "core", [(0, 1), (1, 0)])


def far(values):
    return lax.ppermute(values, "half", [(0, 1), (1, 0)])


def exchange(values):
    return lax.all_to_all(values, ("x", "near"), 0, 0, tiled=True)


def added(*parts):
    return functools.reduce(jnp.add, [p.astype(F32) for p in parts]).astype(BF)


def local(
    prompt_key_matrix,
    prompt_value_matrix,
    response_queries,
    response_cotangent,
    resp_keys,
    resp_values,
    thresholds,
    lengths,
):
    half, near, core = (lax.axis_index(name) for name in ("half", "near", "core"))
    length = lax.dynamic_index_in_dim(lengths, near, 0, keepdims=False)
    where = jnp.stack([half, core, length]).astype(jnp.int32)
    shape = jax.ShapeDtypeStruct
    packed = call(pack_keys_kernel, shape((8, 80, 2 * HD), BF), 4, name="pack_keys")(
        resp_keys, resp_values, prompt_key_matrix, prompt_value_matrix
    )
    keys_own = exchange(packed)
    thresh = jnp.transpose(thresholds.reshape(2, OWN, 4, GROUP), (0, 2, 1, 3))
    rows = call(pack_rows_kernel, shape((8, OWN, PACKED), BF), 3, name="pack_rows")(
        response_queries, response_cotangent, thresh
    )
    keys_far = far(keys_own)
    rows = exchange(rows)
    kvs = [keys_own, swap(keys_own), keys_far, swap(keys_far)]
    outs = attend(where, kvs, rows)
    grads, dq = outs[0:4], outs[4]

    far_sum = added(grads[2], swap(grads[3]))
    key_sum = added(grads[0], swap(grads[1]), far(far_sum))
    back = exchange(jnp.concatenate([dq, key_sum[:, :OWN]], 2))
    prompt_sum = key_sum[:, OWN:].reshape(128, 2 * HD)
    around = [
        lax.ppermute(prompt_sum, "y", [(i, (i + by) % 4) for i in range(4)]) for by in (1, 2, 3)
    ]
    prompt_sum = added(prompt_sum, *around)
    prompt_sum = added(prompt_sum, lax.ppermute(prompt_sum, "hi", [(0, 1), (1, 0)]))
    back, prompt_sum = lax.optimization_barrier((back, prompt_sum))
    prompt_back = exchange(prompt_sum.reshape(8, OWN_PROMPT, 2 * HD))
    grad_queries, grad_resp_keys, grad_resp_values = call(
        unpack_rows_kernel,
        [shape((2, OWN, 4 * WIDE), BF)] + [shape((2, OWN, 4 * HD), BF)] * 2,
        1,
        name="unpack_rows",
    )(back)
    grad_prompt_keys, grad_prompt_values = call(
        unpack_prompt_kernel, [shape((OWN_PROMPT, 4 * HD), BF)] * 2, 1, name="unpack_prompt"
    )(prompt_back)
    return (grad_queries, grad_resp_keys, grad_resp_values, grad_prompt_keys, grad_prompt_values)


def solution(mesh):
    axes = ("y", "hi", "x", "half", "near", "core")
    fine = Mesh(mesh.devices.reshape(4, 2, 4, 2, 2, 2), axes)
    group, line = axes[:2], axes[2:]
    by_row = P(group, line, None)
    return jax.shard_map(
        local,
        mesh=fine,
        in_specs=(P(line, None), P(line, None), by_row, by_row, by_row, by_row, by_row, P(group)),
        out_specs=(by_row, by_row, by_row, P(line, None), P(line, None)),
        check_vma=False,
    )
```

```python
import functools

import jax
import jax.numpy as jnp
from jax import lax
from jax.experimental import pallas as pl
from jax.experimental.pallas import tpu as pltpu
from jax.sharding import Mesh
from jax.sharding import PartitionSpec as P

BF = jnp.bfloat16
F32 = jnp.float32
GROUP = 5
HD = 128
OWN = 64
SPAN = 2 * OWN
ROWS = GROUP * SPAN
WIDE = GROUP * HD
PACKED = 2 * WIDE + HD
PROMPT = 512
OWN_PROMPT = 16
KEYS = PROMPT + 2048
ROOT = HD**0.5
NT = (((1,), (1,)), ((), ()))
NN = (((1,), (0,)), ((), ()))
TN = (((0,), (0,)), ((), ()))


def call(body, out_shape, count, scratch=(), limit=None, name=None, scalars=0, flops=1000):
    vm = pl.BlockSpec(memory_space=pltpu.VMEM)
    return pl.pallas_call(
        body,
        out_shape=out_shape,
        in_specs=[pl.BlockSpec(memory_space=pltpu.SMEM)] * scalars + [vm] * count,
        out_specs=jax.tree.map(lambda _: vm, out_shape),
        scratch_shapes=scratch,
        cost_estimate=pl.CostEstimate(flops=flops, bytes_accessed=2 * 10**6, transcendentals=0),
        compiler_params=pltpu.CompilerParams(vmem_limit_bytes=limit),
        name=name,
    )


def pack_keys_kernel(k_ref, v_ref, pk_ref, pv_ref, out):
    for head in range(4):
        cols = slice(head * HD, (head + 1) * HD)
        for member in range(2):
            to = 2 * head + member
            out[to, 0:OWN, 0:HD] = k_ref[member, :, cols]
            out[to, 0:OWN, HD:] = v_ref[member, :, cols]
            out[to, OWN:, 0:HD] = pk_ref[:, cols]
            out[to, OWN:, HD:] = pv_ref[:, cols]


def pack_rows_kernel(q_ref, c_ref, t_ref, out):
    for head in range(4):
        cols = slice(head * WIDE, (head + 1) * WIDE)
        for member in range(2):
            to = 2 * head + member
            out[to, :, 0:WIDE] = q_ref[member, :, cols]
            out[to, :, WIDE : 2 * WIDE] = c_ref[member, :, cols]
            left = t_ref[member, head]
            for part in range(3):
                piece = left.astype(BF)
                out[to, :, 2 * WIDE + part * GROUP : 2 * WIDE + (part + 1) * GROUP] = piece
                left = left - piece.astype(F32)
            out[to, :, 2 * WIDE + 3 * GROUP :] = jnp.zeros((OWN, HD - 3 * GROUP), BF)


def attend_kernel(step, where, *refs):
    kvs, rows, grads, prompts, dq = refs[0:4], refs[4], refs[5:9], refs[9:11], refs[11]
    k_all, v_all, t_all, q_st, c_st, prob, grad, dk, dv, dq_t = refs[12:]
    half, core, length = where[0], where[1], where[2]

    def key_places(j):
        far, turned = j // 2, j % 2
        base = 256 * (half if far == 0 else 1 - half) + OWN * (core if turned == 0 else 1 - core)
        for e in range(8):
            at = pl.multiple_of(PROMPT + 512 * (e // 2) + SPAN * (e % 2) + base, OWN)
            yield e, pl.ds(at, OWN), pl.ds(OWN_PROMPT * (8 * j + e), OWN_PROMPT)

    for j in range(4):
        for e, at, slot in key_places(j):
            k_all[at] = kvs[j][e, 0:OWN, 0:HD]
            v_all[at] = kvs[j][e, 0:OWN, HD:]
            k_all[slot] = kvs[j][e, OWN:, 0:HD]
            v_all[slot] = kvs[j][e, OWN:, HD:]
    dk[...] = jnp.zeros_like(dk)
    dv[...] = jnp.zeros_like(dv)
    lane = lax.broadcasted_iota(jnp.int32, (1, SPAN), 1)
    origin = 256 * half + OWN * core
    place = jnp.where(lane < OWN, lane, lane + OWN)
    sub = lax.broadcasted_iota(jnp.int32, (512, SPAN), 0)
    barred = jnp.where(sub <= place + origin, 0.0, 1e30)

    def block(b, carry):
        start = b * 512 + origin

        @pl.when(start >= length)
        def _():
            dq[pl.ds(2 * b, 2)] = jnp.zeros((2, OWN, WIDE), BF)

        @pl.when(start < length)
        def _():
            for side in range(2):
                for h in range(GROUP):
                    to = slice(h * SPAN + side * OWN, h * SPAN + (side + 1) * OWN)
                    q_st[to] = rows[2 * b + side, :, h * HD : (h + 1) * HD]
                    c_st[to] = rows[2 * b + side, :, WIDE + h * HD : WIDE + (h + 1) * HD]
            pieces = jnp.concatenate(
                [rows[2 * b + side, :, 2 * WIDE :].astype(F32) for side in range(2)], 0
            ).T
            t_all[...] = (
                pieces[0:GROUP] + pieces[GROUP : 2 * GROUP] + pieces[2 * GROUP : 3 * GROUP]
            ) * ROOT
            live_row = start + place < length
            thr = jnp.concatenate(
                [jnp.where(live_row, t_all[h : h + 1], 1e30) for h in range(GROUP)], 1
            )

            def first(k0, count, bar, totals):
                over = (
                    lax.dot_general(
                        k_all[pl.ds(k0, count)], q_st[...], NT, preferred_element_type=F32
                    )
                    - bar
                )
                weight = jnp.maximum(over, 0.0).astype(BF)
                prob[pl.ds(k0, count)] = weight
                pg = lax.dot_general(
                    v_all[pl.ds(k0, count)], c_st[...], NT, preferred_element_type=F32
                )
                grad[pl.ds(k0, count)] = pg
                live = over > 0.0
                num, tot = totals
                num = num + jnp.sum(jnp.where(live, 1.0, 0.0).reshape(count // 8, 8, ROWS), 0)
                tot = tot + jnp.sum(jnp.where(live, pg, 0.0).reshape(count // 8, 8, ROWS), 0)
                dv[pl.ds(k0, count)] += lax.dot_general(
                    weight, c_st[...], NN, preferred_element_type=F32
                )
                return num, tot

            def main(i, totals):
                return first(pl.multiple_of(i * 2 * step, 2 * step), 2 * step, thr, totals)

            base = PROMPT + b * 512

            def tail(i, totals):
                bar = thr + jnp.concatenate([barred] * GROUP, 1)
                return first(pl.multiple_of(base, 512), 512, bar, totals)

            zero = jnp.zeros((8, ROWS), F32)
            pairs = (1 + b) // 2
            odd = (1 + b) - 2 * pairs
            last = pl.multiple_of(pairs * 2 * step, 2 * step)
            totals = lax.fori_loop(0, pairs, main, (zero, zero))
            totals = lax.fori_loop(0, odd, lambda i, t: first(last, step, thr, t), totals)
            num, tot = tail(0, totals)
            mean = jnp.sum(tot, 0, keepdims=True) / jnp.maximum(
                jnp.sum(num, 0, keepdims=True), 1.0
            )
            dq_t[...] = jnp.zeros_like(dq_t)

            def second(k0, count):
                centred = (grad[pl.ds(k0, count)] - mean).astype(BF)
                ds = jnp.where(prob[pl.ds(k0, count)] > 0, centred, jnp.zeros((), BF))
                dk[pl.ds(k0, count)] += lax.dot_general(
                    ds, q_st[...], NN, preferred_element_type=F32
                )
                dq_t[...] += lax.dot_general(
                    k_all[pl.ds(k0, count)], ds, TN, preferred_element_type=F32
                )

            def main2(i, carry):
                second(pl.multiple_of(i * 2 * step, 2 * step), 2 * step)
                return carry

            def odd2(i, carry):
                second(last, step)
                return carry

            lax.fori_loop(0, pairs, main2, 0)
            lax.fori_loop(0, odd, odd2, 0)
            second(pl.multiple_of(base, 512), 512)
            for h in range(GROUP):
                part = (dq_t[:, h * SPAN : (h + 1) * SPAN].T * (1.0 / ROOT)).astype(BF)
                for side in range(2):
                    dq[2 * b + side, :, h * HD : (h + 1) * HD] = part[side * OWN : (side + 1) * OWN]

        return carry

    lax.fori_loop(0, 4, block, 0)
    for j in range(4):
        for part, total in ((0, dk), (1, dv)):
            cols = slice(part * HD, (part + 1) * HD)
            for e, at, slot in key_places(j):
                grads[j][e, :, cols] = (total[at] * (1.0 / ROOT)).astype(BF)
            held = (total[128 * j : 128 * (j + 1)] * (1.0 / ROOT)).astype(BF)
            prompts[j % 2][j // 2 * 128 : (j // 2 + 1) * 128, cols] = held


def attend(where, kvs, rows):
    shape = jax.ShapeDtypeStruct
    return call(
        functools.partial(attend_kernel, 512),
        [shape((8, OWN, 2 * HD), BF)] * 4
        + [shape((256, 2 * HD), BF)] * 2
        + [shape((8, OWN, WIDE), BF)],
        5,
        [
            pltpu.VMEM((KEYS, HD), BF),
            pltpu.VMEM((KEYS, HD), BF),
            pltpu.VMEM((GROUP, SPAN), F32),
            pltpu.VMEM((ROWS, HD), BF),
            pltpu.VMEM((ROWS, HD), BF),
            pltpu.VMEM((KEYS, ROWS), BF),
            pltpu.VMEM((KEYS, ROWS), F32),
            pltpu.VMEM((KEYS, HD), F32),
            pltpu.VMEM((KEYS, HD), F32),
            pltpu.VMEM((HD, ROWS), F32),
        ],
        48 * 1024 * 1024,
        "attend",
        1,
        6 * 10**9,
    )(where, *kvs, rows)


def unpack_rows_kernel(got, out_q, out_k, out_v):
    for head in range(4):
        cols = slice(head * HD, (head + 1) * HD)
        for member in range(2):
            part = got.at[2 * head + member]
            out_q[member, :, head * WIDE : (head + 1) * WIDE] = part[:, 0:WIDE]
            out_k[member, :, cols] = part[:, WIDE : WIDE + HD]
            out_v[member, :, cols] = part[:, WIDE + HD :]


def unpack_prompt_kernel(got, out_k, out_v):
    for head in range(4):
        cols = slice(head * HD, (head + 1) * HD)
        total = got[2 * head].astype(F32) + got[2 * head + 1].astype(F32)
        out_k[:, cols] = total[:, 0:HD].astype(BF)
        out_v[:, cols] = total[:, HD:].astype(BF)


def swap(values):
    return lax.ppermute(values, "core", [(0, 1), (1, 0)])


def far(values):
    return lax.ppermute(values, "half", [(0, 1), (1, 0)])


def exchange(values):
    return lax.all_to_all(values, ("x", "near"), 0, 0, tiled=True)


def added(*parts):
    return functools.reduce(jnp.add, [p.astype(F32) for p in parts]).astype(BF)


def local(
    prompt_key_matrix,
    prompt_value_matrix,
    response_queries,
    response_cotangent,
    resp_keys,
    resp_values,
    thresholds,
    lengths,
):
    half, near, core = (lax.axis_index(name) for name in ("half", "near", "core"))
    length = lax.dynamic_index_in_dim(lengths, near, 0, keepdims=False)
    where = jnp.stack([half, core, length]).astype(jnp.int32)
    shape = jax.ShapeDtypeStruct
    packed = call(pack_keys_kernel, shape((8, 80, 2 * HD), BF), 4, name="pack_keys")(
        resp_keys, resp_values, prompt_key_matrix, prompt_value_matrix
    )
    keys_own = exchange(packed)
    thresh = jnp.transpose(thresholds.reshape(2, OWN, 4, GROUP), (0, 2, 1, 3))
    rows = call(pack_rows_kernel, shape((8, OWN, PACKED), BF), 3, name="pack_rows")(
        response_queries, response_cotangent, thresh
    )
    keys_far = far(keys_own)
    rows = exchange(rows)
    kvs = [keys_own, swap(keys_own), keys_far, swap(keys_far)]
    outs = attend(where, kvs, rows)
    grads, prompts, dq = outs[0:4], outs[4:6], outs[6]

    far_sum = added(grads[2], swap(grads[3]))
    prompt_sum = added(prompts[0], swap(prompts[1]))
    far_sum, prompt_sum = lax.optimization_barrier((far_sum, prompt_sum))
    key_sum = added(grads[0], swap(grads[1]), far(far_sum))
    corners = [
        lax.ppermute(part, ("hi", "half"), [(i, i ^ mask) for i in range(4)])
        for part, mask in ((prompt_sum[:128], 2), (prompt_sum[128:], 1), (prompt_sum[128:], 3))
    ]
    corners, key_sum = lax.optimization_barrier((corners, key_sum))
    prompt_sum = added(prompt_sum[:128], *corners)
    back = exchange(jnp.concatenate([dq, key_sum], 2))
    around = [
        lax.ppermute(prompt_sum, "y", [(i, (i + by) % 4) for i in range(4)]) for by in (1, 2, 3)
    ]
    prompt_sum = added(prompt_sum, *around).reshape(8, OWN_PROMPT, 2 * HD)
    back, prompt_sum = lax.optimization_barrier((back, prompt_sum))
    prompt_back = exchange(prompt_sum)
    grad_queries, grad_resp_keys, grad_resp_values = call(
        unpack_rows_kernel,
        [shape((2, OWN, 4 * WIDE), BF)] + [shape((2, OWN, 4 * HD), BF)] * 2,
        1,
        name="unpack_rows",
    )(back)
    grad_prompt_keys, grad_prompt_values = call(
        unpack_prompt_kernel, [shape((OWN_PROMPT, 4 * HD), BF)] * 2, 1, name="unpack_prompt"
    )(prompt_back)
    return (grad_queries, grad_resp_keys, grad_resp_values, grad_prompt_keys, grad_prompt_values)


def solution(mesh):
    axes = ("y", "hi", "x", "half", "near", "core")
    fine = Mesh(mesh.devices.reshape(4, 2, 4, 2, 2, 2), axes)
    group, line = axes[:2], axes[2:]
    by_row = P(group, line, None)
    return jax.shard_map(
        local,
        mesh=fine,
        in_specs=(P(line, None), P(line, None), by_row, by_row, by_row, by_row, by_row, P(group)),
        out_specs=(by_row, by_row, by_row, P(line, None), P(line, None)),
        check_vma=False,
    )
```

```python
import functools

import jax
import jax.numpy as jnp
from jax import lax
from jax.experimental import pallas as pl
from jax.experimental.pallas import tpu as pltpu
from jax.sharding import Mesh
from jax.sharding import PartitionSpec as P

BF = jnp.bfloat16
F32 = jnp.float32
GROUP = 5
HD = 128
OWN = 64
SPAN = 2 * OWN
ROWS = GROUP * SPAN
WIDE = GROUP * HD
PACKED = 2 * WIDE + HD
PROMPT = 512
OWN_PROMPT = 16
KEYS = PROMPT + 2048
ROOT = HD**0.5
NT = (((1,), (1,)), ((), ()))
NN = (((1,), (0,)), ((), ()))
TN = (((0,), (0,)), ((), ()))


def call(body, out_shape, count, scratch=(), limit=None, name=None, scalars=0, flops=1000):
    vm = pl.BlockSpec(memory_space=pltpu.VMEM)
    return pl.pallas_call(
        body,
        out_shape=out_shape,
        in_specs=[pl.BlockSpec(memory_space=pltpu.SMEM)] * scalars + [vm] * count,
        out_specs=jax.tree.map(lambda _: vm, out_shape),
        scratch_shapes=scratch,
        cost_estimate=pl.CostEstimate(flops=flops, bytes_accessed=2 * 10**6, transcendentals=0),
        compiler_params=pltpu.CompilerParams(vmem_limit_bytes=limit),
        name=name,
    )


def pack_keys_kernel(k_ref, v_ref, pk_ref, pv_ref, out):
    for head in range(4):
        cols = slice(head * HD, (head + 1) * HD)
        for member in range(2):
            to = 2 * head + member
            out[to, 0:OWN, 0:HD] = k_ref[member, :, cols]
            out[to, 0:OWN, HD:] = v_ref[member, :, cols]
            out[to, OWN:, 0:HD] = pk_ref[:, cols]
            out[to, OWN:, HD:] = pv_ref[:, cols]


def pack_rows_kernel(q_ref, c_ref, t_ref, out):
    for head in range(4):
        cols = slice(head * WIDE, (head + 1) * WIDE)
        for member in range(2):
            to = 2 * head + member
            out[to, :, 0:WIDE] = q_ref[member, :, cols]
            out[to, :, WIDE : 2 * WIDE] = c_ref[member, :, cols]
            left = t_ref[member, head]
            for part in range(3):
                piece = left.astype(BF)
                out[to, :, 2 * WIDE + part * GROUP : 2 * WIDE + (part + 1) * GROUP] = piece
                left = left - piece.astype(F32)
            out[to, :, 2 * WIDE + 3 * GROUP :] = jnp.zeros((OWN, HD - 3 * GROUP), BF)


def attend_kernel(step, where, *refs):
    kvs, rows, grads, prompts, dq = refs[0:4], refs[4], refs[5:9], refs[9:11], refs[11]
    k_all, v_all, t_all, q_st, c_st, prob, grad, dk, dv, dq_t = refs[12:]
    half, core, length = where[0], where[1], where[2]

    def key_places(j):
        far, turned = j // 2, j % 2
        base = 256 * (half if far == 0 else 1 - half) + OWN * (core if turned == 0 else 1 - core)
        for e in range(8):
            at = pl.multiple_of(PROMPT + 512 * (e // 2) + SPAN * (e % 2) + base, OWN)
            yield e, pl.ds(at, OWN), pl.ds(OWN_PROMPT * (8 * j + e), OWN_PROMPT)

    for j in range(4):
        for e, at, slot in key_places(j):
            k_all[at] = kvs[j][e, 0:OWN, 0:HD]
            v_all[at] = kvs[j][e, 0:OWN, HD:]
            k_all[slot] = kvs[j][e, OWN:, 0:HD]
            v_all[slot] = kvs[j][e, OWN:, HD:]
    dk[...] = jnp.zeros_like(dk)
    dv[...] = jnp.zeros_like(dv)
    lane = lax.broadcasted_iota(jnp.int32, (1, SPAN), 1)
    origin = 256 * half + OWN * core
    place = jnp.where(lane < OWN, lane, lane + OWN)
    sub = lax.broadcasted_iota(jnp.int32, (512, SPAN), 0)
    barred = jnp.where(sub <= place + origin, 0.0, 1e30)

    def block(b, carry):
        start = b * 512 + origin

        @pl.when(start >= length)
        def _():
            dq[pl.ds(2 * b, 2)] = jnp.zeros((2, OWN, WIDE), BF)

        @pl.when(start < length)
        def _():
            for side in range(2):
                for h in range(GROUP):
                    to = slice(h * SPAN + side * OWN, h * SPAN + (side + 1) * OWN)
                    q_st[to] = rows[2 * b + side, :, h * HD : (h + 1) * HD]
                    c_st[to] = rows[2 * b + side, :, WIDE + h * HD : WIDE + (h + 1) * HD]
            pieces = jnp.concatenate(
                [rows[2 * b + side, :, 2 * WIDE :].astype(F32) for side in range(2)], 0
            ).T
            t_all[...] = (
                pieces[0:GROUP] + pieces[GROUP : 2 * GROUP] + pieces[2 * GROUP : 3 * GROUP]
            ) * ROOT
            live_row = start + place < length
            thr = jnp.concatenate(
                [jnp.where(live_row, t_all[h : h + 1], 1e30) for h in range(GROUP)], 1
            )

            def first(k0, count, bar, totals):
                over = (
                    lax.dot_general(
                        k_all[pl.ds(k0, count)], q_st[...], NT, preferred_element_type=F32
                    )
                    - bar
                )
                weight = jnp.maximum(over, 0.0).astype(BF)
                prob[pl.ds(k0, count)] = weight
                pg = lax.dot_general(
                    v_all[pl.ds(k0, count)], c_st[...], NT, preferred_element_type=F32
                )
                grad[pl.ds(k0, count)] = pg
                live = over > 0.0
                num, tot = totals
                num = num + jnp.sum(jnp.where(live, 1.0, 0.0).reshape(count // 8, 8, ROWS), 0)
                tot = tot + jnp.sum(jnp.where(live, pg, 0.0).reshape(count // 8, 8, ROWS), 0)
                dv[pl.ds(k0, count)] += lax.dot_general(
                    weight, c_st[...], NN, preferred_element_type=F32
                )
                return num, tot

            def main(i, totals):
                return first(pl.multiple_of(i * 2 * step, 2 * step), 2 * step, thr, totals)

            base = PROMPT + b * 512

            def tail(i, totals):
                bar = thr + jnp.concatenate([barred] * GROUP, 1)
                return first(pl.multiple_of(base, 512), 512, bar, totals)

            zero = jnp.zeros((8, ROWS), F32)
            pairs = (1 + b) // 2
            odd = (1 + b) - 2 * pairs
            last = pl.multiple_of(pairs * 2 * step, 2 * step)
            totals = lax.fori_loop(0, pairs, main, (zero, zero))
            totals = lax.fori_loop(0, odd, lambda i, t: first(last, step, thr, t), totals)
            num, tot = tail(0, totals)
            mean = jnp.sum(tot, 0, keepdims=True) / jnp.maximum(
                jnp.sum(num, 0, keepdims=True), 1.0
            )
            dq_t[...] = jnp.zeros_like(dq_t)

            def second(k0, count):
                centred = (grad[pl.ds(k0, count)] - mean).astype(BF)
                ds = jnp.where(prob[pl.ds(k0, count)] > 0, centred, jnp.zeros((), BF))
                dk[pl.ds(k0, count)] += lax.dot_general(
                    ds, q_st[...], NN, preferred_element_type=F32
                )
                dq_t[...] += lax.dot_general(
                    k_all[pl.ds(k0, count)], ds, TN, preferred_element_type=F32
                )

            def main2(i, carry):
                second(pl.multiple_of(i * 2 * step, 2 * step), 2 * step)
                return carry

            def odd2(i, carry):
                second(last, step)
                return carry

            lax.fori_loop(0, pairs, main2, 0)
            lax.fori_loop(0, odd, odd2, 0)
            second(pl.multiple_of(base, 512), 512)
            for h in range(GROUP):
                part = (dq_t[:, h * SPAN : (h + 1) * SPAN].T * (1.0 / ROOT)).astype(BF)
                for side in range(2):
                    dq[2 * b + side, :, h * HD : (h + 1) * HD] = part[side * OWN : (side + 1) * OWN]

        return carry

    lax.fori_loop(0, 4, block, 0)
    for j in range(4):
        for part, total in ((0, dk), (1, dv)):
            cols = slice(part * HD, (part + 1) * HD)
            for e, at, slot in key_places(j):
                grads[j][e, :, cols] = (total[at] * (1.0 / ROOT)).astype(BF)
            held = (total[128 * j : 128 * (j + 1)] * (1.0 / ROOT)).astype(BF)
            prompts[j % 2][j // 2 * 128 : (j // 2 + 1) * 128, cols] = held


def attend(where, kvs, rows):
    shape = jax.ShapeDtypeStruct
    return call(
        functools.partial(attend_kernel, 512),
        [shape((8, OWN, 2 * HD), BF)] * 4
        + [shape((256, 2 * HD), BF)] * 2
        + [shape((8, OWN, WIDE), BF)],
        5,
        [
            pltpu.VMEM((KEYS, HD), BF),
            pltpu.VMEM((KEYS, HD), BF),
            pltpu.VMEM((GROUP, SPAN), F32),
            pltpu.VMEM((ROWS, HD), BF),
            pltpu.VMEM((ROWS, HD), BF),
            pltpu.VMEM((KEYS, ROWS), BF),
            pltpu.VMEM((KEYS, ROWS), F32),
            pltpu.VMEM((KEYS, HD), F32),
            pltpu.VMEM((KEYS, HD), F32),
            pltpu.VMEM((HD, ROWS), F32),
        ],
        48 * 1024 * 1024,
        "attend",
        1,
        6 * 10**9,
    )(where, *kvs, rows)


def unpack_rows_kernel(got, out_q, out_k, out_v):
    for head in range(4):
        cols = slice(head * HD, (head + 1) * HD)
        for member in range(2):
            part = got.at[2 * head + member]
            out_q[member, :, head * WIDE : (head + 1) * WIDE] = part[:, 0:WIDE]
            out_k[member, :, cols] = part[:, WIDE : WIDE + HD]
            out_v[member, :, cols] = part[:, WIDE + HD :]


def swap(values):
    return lax.ppermute(values, "core", [(0, 1), (1, 0)])


def far(values):
    return lax.ppermute(values, "half", [(0, 1), (1, 0)])


def exchange(values):
    return lax.all_to_all(values, ("x", "near"), 0, 0, tiled=True)


def added(*parts):
    return functools.reduce(jnp.add, [p.astype(F32) for p in parts]).astype(BF)


def local(
    prompt_key_matrix,
    prompt_value_matrix,
    response_queries,
    response_cotangent,
    resp_keys,
    resp_values,
    thresholds,
    lengths,
):
    half, near, core = (lax.axis_index(name) for name in ("half", "near", "core"))
    length = lax.dynamic_index_in_dim(lengths, near, 0, keepdims=False)
    where = jnp.stack([half, core, length]).astype(jnp.int32)
    shape = jax.ShapeDtypeStruct
    packed = call(pack_keys_kernel, shape((8, 80, 2 * HD), BF), 4, name="pack_keys")(
        resp_keys, resp_values, prompt_key_matrix, prompt_value_matrix
    )
    keys_own = exchange(packed)
    thresh = jnp.transpose(thresholds.reshape(2, OWN, 4, GROUP), (0, 2, 1, 3))
    rows = call(pack_rows_kernel, shape((8, OWN, PACKED), BF), 3, name="pack_rows")(
        response_queries, response_cotangent, thresh
    )
    keys_far = far(keys_own)
    rows = exchange(rows)
    kvs = [keys_own, swap(keys_own), keys_far, swap(keys_far)]
    outs = attend(where, kvs, rows)
    grads, prompts, dq = outs[0:4], outs[4:6], outs[6]

    far_sum = added(grads[2], swap(grads[3]))
    prompt_sum = added(prompts[0], swap(prompts[1]))
    far_sum, prompt_sum = lax.optimization_barrier((far_sum, prompt_sum))
    key_sum = added(grads[0], swap(grads[1]), far(far_sum))
    corners = [
        lax.ppermute(part, ("hi", "half"), [(i, i ^ mask) for i in range(4)])
        for part, mask in ((prompt_sum[:128], 2), (prompt_sum[128:], 1), (prompt_sum[128:], 3))
    ]
    corners, key_sum = lax.optimization_barrier((corners, key_sum))
    prompt_sum = added(prompt_sum[:128], *corners)
    back = exchange(jnp.concatenate([dq, key_sum], 2))
    around = [
        lax.ppermute(prompt_sum, "y", [(i, (i + by) % 4) for i in range(4)]) for by in (1, 2, 3)
    ]
    prompt_sum = added(prompt_sum, *around).reshape(8, OWN_PROMPT, 2 * HD)
    back, prompt_sum = lax.optimization_barrier((back, prompt_sum))
    prompt_back = exchange(prompt_sum)
    grad_queries, grad_resp_keys, grad_resp_values = call(
        unpack_rows_kernel,
        [shape((2, OWN, 4 * WIDE), BF)] + [shape((2, OWN, 4 * HD), BF)] * 2,
        1,
        name="unpack_rows",
    )(back)
    total = prompt_back.reshape(4, 2, OWN_PROMPT, 2 * HD).astype(F32)
    total = (total[:, 0] + total[:, 1]).astype(BF)
    total = jnp.concatenate([total[head] for head in range(4)], 1).reshape(OWN_PROMPT, 4, 2, HD)
    grad_prompt_keys = total[:, :, 0].reshape(OWN_PROMPT, 4 * HD)
    grad_prompt_values = total[:, :, 1].reshape(OWN_PROMPT, 4 * HD)
    return (grad_queries, grad_resp_keys, grad_resp_values, grad_prompt_keys, grad_prompt_values)


def solution(mesh):
    axes = ("y", "hi", "x", "half", "near", "core")
    fine = Mesh(mesh.devices.reshape(4, 2, 4, 2, 2, 2), axes)
    group, line = axes[:2], axes[2:]
    by_row = P(group, line, None)
    return jax.shard_map(
        local,
        mesh=fine,
        in_specs=(P(line, None), P(line, None), by_row, by_row, by_row, by_row, by_row, P(group)),
        out_specs=(by_row, by_row, by_row, P(line, None), P(line, None)),
        check_vma=False,
    )
```
